32 devices in a mesh: groups: 2 (over x), context: 16 (over z, y, core).
Axes of the slice: x: 2, y: 2, z: 4, core: 2. Of those that a mesh axis runs over, the one named last changes fastest.
Arguments:
- queries: bfloat16 [4096, 16, 128], P(('groups', 'context')), parts along dimension 0, may hold values from -24 to 24
- keys: bfloat16 [4096, 8, 128], P(('groups', 'context')), parts along dimension 0, may hold values from -24 to 24
- values: bfloat16 [4096, 8, 128], P(('groups', 'context')), parts along dimension 0, may hold values from -6 to 6
- grad_out: bfloat16 [4096, 16, 128], P(('groups', 'context')), parts along dimension 0, may hold values from -24 to 24
- readout: float32 [16, 128], replicated, may hold values from -4 to 4
- segments: int32 [4096], P(('groups', 'context')), parts along dimension 0, may hold values from 0 to 3, never falling along the last dimension, each value on 1 to 1024 neighbouring positions
- loss_mask: int32 [4096], P(('groups', 'context')), parts along dimension 0, may hold values from 0 to 1, as said below
- labels: int32 [4096], P(('groups', 'context')), parts along dimension 0, may hold values 0 or 1
Outputs:
- grad_queries: bfloat16 [4096, 16, 128], P(('groups', 'context')), parts along dimension 0
- grad_keys: bfloat16 [4096, 8, 128], P(('groups', 'context')), parts along dimension 0
- grad_values: bfloat16 [4096, 8, 128], P(('groups', 'context')), parts along dimension 0
The draws below stay inside these ranges and needn't reach their ends.
There are 2 independent parts, one for each index of `groups`. The reference program is written for one: setup_inputs(seed, part) draws one part's arguments, and reference() takes and returns one part's arrays. A program takes and returns all parts, laid end to end along the dimension named above; an argument that names none is the same for every part. Nothing has to cross between parts.
Inputs may be any that keep to these rules, and one draw needn't show every extreme that they name: `loss_mask`: every entry of the first 128 positions is 0.
All inputs are finite; a program needn't handle non-finite values. No bound on the sum of `labels` on one device may be relied on, other than what follows from the above.
Results may differ from the reference program's by a relative error of at most 0.025.
Values may be sent and summed in bfloat16 or wider, within the bound.
A program may use at most 128 MiB of HBM per device.

```python
import math
import jax
import jax.numpy as jnp
import numpy as np
from jax import lax

HEADS = 16
KV_HEADS = 8
HEAD_DIM = 128
WINDOW = 1024
TOK_DEV = 128
TOKENS = 2048
DOCS = 4
DOC_MOST = 1024


def drawn_rows(key, salt, head_count):
    inner = jax.random.fold_in(key, salt)
    return jax.random.truncated_normal(inner, -4.0, 4.0, (TOKENS, head_count, HEAD_DIM), jnp.float32)


def draw_queries(key, part):
    base = drawn_rows(key, 1, HEADS)
    return base.astype(jnp.bfloat16)


def draw_keys(key, part):
    base = drawn_rows(key, 2, KV_HEADS)
    return base.astype(jnp.bfloat16)


def draw_loss_mask(key, part):
    first, second = jax.random.split(jax.random.fold_in(key, 5))
    block_count = TOKENS // TOK_DEV
    live_blocks = jax.random.randint(first, (block_count,), 0, 4) > 0
    live_blocks = jnp.where(jnp.arange(block_count) == 0, False, live_blocks)
    token_live = jax.random.randint(second, (TOKENS,), 0, 5) < 3
    return (jnp.repeat(live_blocks, TOK_DEV) & token_live).astype(jnp.int32)


def plant(values, own_key, smallest, high):
    dims = values.shape
    place = [jax.random.randint(jax.random.fold_in(own_key, axis), (), 0, dims[axis]) for axis in range(len(dims))]
    values = values.at[tuple(place)].set(smallest)
    longest = dims.index(max(dims))
    place[longest] = (place[longest] + 1) % dims[longest]
    return values.at[tuple(place)].set(high)


def level_of(rng, dims, cuts, least, high):
    def one(position, parts):
        steps = jax.random.uniform(jax.random.fold_in(jax.random.fold_in(rng, 6), position), (parts,), jnp.float32, least / len(cuts), high / len(cuts))
        return jnp.repeat(jnp.exp(steps), dims[position] // parts).reshape((-1,) + (1,) * (len(dims) - position - 1))

    gain = one(*cuts[0])
    for cut in cuts[1:]:
        gain = gain * one(*cut)
    return gain


def split_up(amount, total, limit, skew):
    loads = [(1 << 20) // math.isqrt(rank ** skew) + 1 for rank in range(2, amount + 1)]
    rest, given = total - limit - (amount - 1), [1] * (amount - 1)
    while rest > 0:
        candidates = [i for i in range(amount - 1) if given[i] < limit]
        mass, remaining = sum([loads[i] for i in candidates]), rest
        for i in candidates:
            extra = min(limit - given[i], max(1, remaining * loads[i] // mass), rest)
            given[i] = given[i] + extra
            rest = rest - extra
    return np.array([limit] + given)


def ragged_sizes(stream_key, amount, total, most, skew):
    if amount == 2:
        one = jax.random.randint(stream_key, (), max(1, total - most), min(most, total - 1) + 1)
        return jnp.stack([one, total - one])
    lengths = jnp.asarray(split_up(amount, total, most, skew), jnp.int32)
    pairs = (amount - 1) // 2
    donor, taker = lengths[1:1 + 2 * pairs:2], lengths[2:2 + 2 * pairs:2]
    slack = jnp.minimum(donor - 1, most - taker)
    passed = jax.random.randint(jax.random.fold_in(stream_key, 1), (pairs,), 0, 1 << 20) % (slack + 1)
    lengths = lengths.at[1:1 + 2 * pairs:2].set(donor - passed).at[2:2 + 2 * pairs:2].set(taker + passed)
    return lengths[jax.random.permutation(jax.random.fold_in(stream_key, 2), amount)]


def normal_values(stream_key, extent, scale, bound, cuts=(), kind=jnp.bfloat16):
    level = level_of(stream_key, extent, cuts, -0.22, 0.18) if cuts else 1.0
    drawn = jax.random.normal(stream_key, extent, jnp.float32) * scale * level
    return jnp.minimum(jnp.maximum(drawn, -bound), bound).astype(kind)


def setup_inputs(seed: int = 0, part: int = 0) -> dict:
    streams_of = jax.random.split(jax.random.key(seed), 9)
    part_keys = jax.random.split(jax.random.fold_in(streams_of[8], part), 9)
    return {
        "queries": draw_queries(jax.random.fold_in(jax.random.fold_in(streams_of[8], part), 71), part),
        "keys": draw_keys(jax.random.fold_in(jax.random.fold_in(streams_of[8], part), 71), part),
        "values": normal_values(part_keys[2], (TOKENS, KV_HEADS, HEAD_DIM), 1.0, 6.0, ((0, 16),)),
        "grad_out": normal_values(part_keys[3], (TOKENS, HEADS, HEAD_DIM), 4.0, 24.0, ((0, 16),)),
        "readout": normal_values(streams_of[4], (HEADS, HEAD_DIM), 1.0, 4.0, (), jnp.float32),
        "segments": jnp.searchsorted(jnp.cumsum(ragged_sizes(part_keys[5], DOCS, TOKENS, DOC_MOST, 1)), jnp.arange(TOKENS), side="right").astype(jnp.int32),
        "loss_mask": draw_loss_mask(jax.random.fold_in(jax.random.fold_in(streams_of[8], part), 71), part),
        "labels": plant((jax.random.randint(part_keys[7], (TOKENS,), 0, 2) < 1).astype(jnp.int32), jax.random.fold_in(part_keys[7], 1), 0, 1),
    }


SCALE = 168.0 ** -0.5
NEGATIVE = -1e30


def block_inputs(block_id, queries, key_pad, value_pad, segments, seg_pad):
    start = (block_id * TOK_DEV).astype(jnp.int32)
    query_part = lax.dynamic_slice_in_dim(queries, start, TOK_DEV, 0)
    key_part = lax.dynamic_slice_in_dim(key_pad, start, TOK_DEV + WINDOW, 0)
    value_part = lax.dynamic_slice_in_dim(value_pad, start, TOK_DEV + WINDOW, 0)
    seg_query = lax.dynamic_slice_in_dim(segments, start, TOK_DEV, 0)
    seg_key = lax.dynamic_slice_in_dim(seg_pad, start, TOK_DEV + WINDOW, 0)
    query_pos = start + jnp.arange(TOK_DEV, dtype=jnp.int32)
    key_pos = start - WINDOW + jnp.arange(TOK_DEV + WINDOW, dtype=jnp.int32)
    distance = query_pos[:, None] - key_pos[None, :]
    allowed = (distance >= 0) & (distance < WINDOW) & (key_pos[None, :] >= 0) & (seg_query[:, None] == seg_key[None, :])
    return start, query_part, key_part, value_part, allowed


def grouped(array):
    return array.reshape(array.shape[0], KV_HEADS, HEADS // KV_HEADS, HEAD_DIM).astype(jnp.float32)


def probabilities(query_part, key_part, allowed):
    scores = jnp.einsum("qgrd,kgd->grqk", grouped(query_part), key_part.astype(jnp.float32)) * SCALE
    mask = allowed[None, None]
    scores = jnp.where(mask, scores, NEGATIVE)
    row_max = jnp.max(scores, axis=-1, keepdims=True)
    row_total = jnp.sum(jnp.where(mask, jnp.exp(scores - row_max), 0.0), axis=-1, keepdims=True)
    log_total = row_max + jnp.log(row_total)
    return jnp.where(mask, jnp.exp(scores - log_total), 0.0)


def reference(queries, keys, values, grad_out, readout, segments, loss_mask, labels):
    blocks = TOKENS // TOK_DEV
    key_pad = jnp.concatenate([jnp.zeros((WINDOW, KV_HEADS, HEAD_DIM), keys.dtype), keys], axis=0)
    value_pad = jnp.concatenate([jnp.zeros((WINDOW, KV_HEADS, HEAD_DIM), values.dtype), values], axis=0)
    seg_pad = jnp.concatenate([jnp.full((WINDOW,), -1, jnp.int32), segments.astype(jnp.int32)], axis=0)
    block_ids = jnp.arange(blocks, dtype=jnp.int32)

    def forward(block_id):
        start, query_part, key_part, value_part, allowed = block_inputs(block_id, queries, key_pad, value_pad, segments, seg_pad)
        prob = probabilities(query_part, key_part, allowed)
        prob_low = prob.astype(jnp.bfloat16)
        out = jnp.einsum("grqk,kgd->qgrd", prob_low.astype(jnp.float32), value_part.astype(jnp.float32))
        return out.reshape(TOK_DEV, HEADS, HEAD_DIM)

    attn_out = lax.map(forward, block_ids).reshape(TOKENS, HEADS, HEAD_DIM)
    reward = jnp.sum(attn_out * readout[None], axis=(1, 2))
    live_rows = loss_mask.astype(jnp.float32)
    probe_grad = live_rows * (jax.nn.sigmoid(reward) - labels.astype(jnp.float32))
    grad_attn = (live_rows[:, None, None] * grad_out.astype(jnp.float32) + probe_grad[:, None, None] * readout[None]).astype(jnp.bfloat16)
    delta = jnp.sum(grad_attn.astype(jnp.float32) * attn_out, axis=-1)

    def backward(carry, block_id):
        key_acc, value_acc = carry
        start, query_part, key_part, value_part, allowed = block_inputs(block_id, queries, key_pad, value_pad, segments, seg_pad)
        prob = probabilities(query_part, key_part, allowed)
        prob_low = prob.astype(jnp.bfloat16)
        grad_part = grouped(lax.dynamic_slice_in_dim(grad_attn, start, TOK_DEV, 0))
        delta_part = lax.dynamic_slice_in_dim(delta, start, TOK_DEV, 0).reshape(TOK_DEV, KV_HEADS, HEADS // KV_HEADS)
        grad_prob = jnp.einsum("qgrd,kgd->grqk", grad_part, value_part.astype(jnp.float32))
        grad_score = (prob * (grad_prob - jnp.transpose(delta_part, (1, 2, 0))[..., None])).astype(jnp.bfloat16)
        query_grad = (jnp.einsum("grqk,kgd->qgrd", grad_score.astype(jnp.float32), key_part.astype(jnp.float32)) * SCALE).astype(jnp.bfloat16)
        key_term = jnp.einsum("grqk,qgrd->kgd", grad_score.astype(jnp.float32), grouped(query_part)) * SCALE
        value_term = jnp.einsum("grqk,qgrd->kgd", prob_low.astype(jnp.float32), grad_part)
        old_keys = lax.dynamic_slice_in_dim(key_acc, start, TOK_DEV + WINDOW, 0)
        old_values = lax.dynamic_slice_in_dim(value_acc, start, TOK_DEV + WINDOW, 0)
        zero = jnp.zeros((), jnp.int32)
        key_acc = lax.dynamic_update_slice(key_acc, old_keys + key_term, (start, zero, zero))
        value_acc = lax.dynamic_update_slice(value_acc, old_values + value_term, (start, zero, zero))
        return (key_acc, value_acc), query_grad.reshape(TOK_DEV, HEADS, HEAD_DIM)

    empty = jnp.zeros((TOKENS + WINDOW, KV_HEADS, HEAD_DIM), jnp.float32)
    (key_acc, value_acc), query_grads = lax.scan(backward, (empty, empty), block_ids)
    grad_queries = query_grads.reshape(TOKENS, HEADS, HEAD_DIM)
    grad_keys = key_acc[WINDOW:].astype(jnp.bfloat16)
    grad_values = value_acc[WINDOW:].astype(jnp.bfloat16)
    return (grad_queries, grad_keys, grad_values)
```

```python
import functools

import jax
import jax.numpy as jnp
from jax import lax
from jax.experimental import pallas as pl
from jax.experimental.pallas import tpu as pltpu
from jax.sharding import PartitionSpec as P

WINDOW = 1024
SCALE = 168.0 ** (-0.5)
NEGATIVE = -1e30
MESH = pl.DeviceIdType.MESH
R = 4
T = 128
D = 128
BF = jnp.bfloat16
F32 = jnp.float32
KV_A, QG_A, ME_A, KV_1, ME_1, KV_2, ME_2, RW, B2, B1, OQ, OKV = range(12)


def dot(a, b, ca, cb):
    return lax.dot_general(a, b, (((ca,), (cb,)), ((), ())), preferred_element_type=F32)


def kernel(
    n, kv_in, qg_in, me_in, ro_ref, oq, okv,
    kvb, qgb, meta, segc, rob, bias, pb, ob, rwb, acc, gqb, b2s, b2r, b1s, b1r, kvs,
    ssem, rsem,
):
    planes = n // R
    me = lax.axis_index("context")
    r = lax.rem(me, R)
    p = lax.div(me, R)
    base = p * R
    has_dn = p >= 1
    has_up = p < planes - 1
    has2 = p >= 2
    mid = jnp.logical_and(has_dn, has_up)
    up = me + R
    dn = me - R

    def send(k, src, dst, to, s, d):
        pltpu.make_async_remote_copy(
            src_ref=src, dst_ref=dst, send_sem=ssem.at[k, s], recv_sem=rsem.at[k, d],
            device_id={"context": to}, device_id_type=MESH,
        ).start()

    def wait_recv(k, c, ref):
        pltpu.make_async_copy(ref, ref, rsem.at[k, c]).wait()

    def wait_send(k, c, ref):
        pltpu.make_async_copy(ref, ref, ssem.at[k, c]).wait()

    def peer(o):
        return lax.rem(r + o, R)

    def rows(start):
        return pl.ds(pl.multiple_of(start, T), T)

    def kchunk(c):
        return kvb.at[rows(c * T)]

    def qchunk(c):
        return qgb.at[rows(c * T)]

    barrier = pltpu.get_barrier_semaphore()
    for o in range(1, R):
        pl.semaphore_signal(barrier, inc=1, device_id={"context": base + peer(o)}, device_id_type=MESH)

    @pl.when(has_dn)
    def _():
        pl.semaphore_signal(barrier, inc=1, device_id={"context": dn}, device_id_type=MESH)

    @pl.when(has_up)
    def _():
        pl.semaphore_signal(barrier, inc=1, device_id={"context": up}, device_id_type=MESH)

    pltpu.make_async_copy(kv_in.at[r], kchunk(8 + r), rsem.at[KV_A, r]).start()
    pltpu.make_async_copy(me_in, meta.at[8 + r], rsem.at[ME_A, r]).start()
    pltpu.make_async_copy(qg_in.at[r], qchunk(r), rsem.at[QG_A, r]).start()
    pl.semaphore_wait(barrier, R - 1 + has_dn.astype(jnp.int32) + has_up.astype(jnp.int32))

    for o in range(1, R):
        d = peer(o)
        send(KV_A, kv_in.at[d], kchunk(8 + r), base + d, d, r)
        send(ME_A, me_in, meta.at[8 + r], base + d, d, r)
    for o in range(1, R):
        d = peer(o)
        send(QG_A, qg_in.at[d], qchunk(r), base + d, d, r)

    for c in range(R - 1, -1, -1):
        wait_recv(KV_A, c, kchunk(8 + c))
        wait_recv(ME_A, c, meta.at[8 + c])

        @pl.when(has_up)
        def _():
            send(KV_1, kchunk(8 + c), kchunk(4 + c), up, c, c)
            send(ME_1, meta.at[8 + c], meta.at[4 + c], up, c, c)

    @pl.when(jnp.logical_not(has_dn))
    def _():
        kvb[4 * T : 8 * T] = jnp.zeros((4 * T, 4 * D), BF)
        meta[4:8] = jnp.full((4, 8, T), -1.0, F32)

    @pl.when(jnp.logical_not(has2))
    def _():
        kvb[0 : 4 * T] = jnp.zeros((4 * T, 4 * D), BF)
        meta[0:4] = jnp.full((4, 8, T), -1.0, F32)

    acc[...] = jnp.zeros_like(acc)
    for h in range(4):
        rob[h] = jnp.broadcast_to(ro_ref[pl.ds(4 * r + h, 1), :], (D, D)).T

    for c in range(R - 1, -1, -1):
        @pl.when(has_dn)
        def _():
            wait_recv(KV_1, c, kchunk(4 + c))
            wait_recv(ME_1, c, meta.at[4 + c])

        @pl.when(mid)
        def _():
            send(KV_2, kchunk(4 + c), kchunk(c), up, c, c)
            send(ME_2, meta.at[4 + c], meta.at[c], up, c, c)

    for c in range(R):
        wait_recv(QG_A, c, qchunk(c))

    def seg_column(c):
        segc[rows(c * T)] = jnp.broadcast_to(meta[c, 0:1, :], (T, T)).T

    def seg_body(c, carry):
        seg_column(c + 4)
        return carry

    lax.fori_loop(0, 8, seg_body, 0)

    def win(i):
        return pl.ds(pl.multiple_of(i * T, T), WINDOW + T)

    def two(ref, i, g, at):
        lane = at + 2 * g * D
        return jnp.concatenate(
            [ref[rows(i * T), lane : lane + D], ref[rows(i * T), lane + D : lane + 2 * D]], axis=0
        )

    def forward(step, carry):
        i = R - 1 - step

        @pl.when(has2)
        def _():
            wait_recv(KV_2, i, kchunk(i))
            wait_recv(ME_2, i, meta.at[i])

        seg_column(i)
        seg_q = meta[8 + i, 0:1, :]
        for j in range(9):
            ok = segc[rows((i + j) * T)] == seg_q
            if j in (0, 8):
                kk = lax.broadcasted_iota(jnp.int32, (T, T), 0)
                tq = lax.broadcasted_iota(jnp.int32, (T, T), 1)
                ok = jnp.logical_and(ok, kk > tq if j == 0 else kk <= tq)
            bias[j * T : (j + 1) * T] = jnp.where(ok, 0.0, NEGATIVE)
        total = jnp.zeros((1, T), F32)
        for g in range(2):
            q2 = two(qgb, i, g, 0)
            s = dot(kvb[win(i), g * D : (g + 1) * D], q2, 1, 1) * SCALE
            b = bias[...]
            s = s + jnp.concatenate([b, b], axis=1)
            e = jnp.exp(s - jnp.max(s, axis=0, keepdims=True))
            low = (e * (1.0 / jnp.sum(e, axis=0, keepdims=True))).astype(BF)
            pb[2 * i + g] = low
            o = dot(kvb[win(i), (2 + g) * D : (3 + g) * D], low, 0, 0)
            ob[2 * i + g] = o
            w = o[:, :T] * rob[2 * g] + o[:, T:] * rob[2 * g + 1]
            total = total + jnp.sum(w, axis=0, keepdims=True)
        rwb[r, i] = jnp.broadcast_to(total, (8, T))
        return carry

    lax.fori_loop(0, R, forward, 0)

    for o in range(1, R):
        send(RW, rwb.at[r], rwb.at[r], base + peer(o), peer(o), r)
    for o in range(1, R):
        wait_recv(RW, peer(o), rwb.at[peer(o)])

    def packed(start):
        return jnp.concatenate(
            [acc[rows(start), : 2 * D] * SCALE, acc[rows(start), 2 * D :]], axis=1
        )

    def backward(i, carry):
        reward = jnp.sum(rwb[:, i, 0:1, :], axis=0)
        live = meta[8 + i, 1:2, :]
        pg = live * (jax.nn.sigmoid(reward) - meta[8 + i, 2:3, :])
        for g in range(2):
            q2 = two(qgb, i, g, 0)
            go = two(qgb, i, g, 4 * D).astype(F32).T
            ga_t = jnp.concatenate(
                [
                    live * go[:, :T] + pg * rob[2 * g],
                    live * go[:, T:] + pg * rob[2 * g + 1],
                ],
                axis=1,
            ).astype(BF)
            ga_f = ga_t.astype(F32)
            ga2 = ga_f.T.astype(BF)
            delta = jnp.sum(ga_f * ob[2 * i + g], axis=0, keepdims=True)
            low = pb[2 * i + g]
            dp = dot(kvb[win(i), (2 + g) * D : (3 + g) * D], ga_t, 1, 0)
            ds = (low.astype(F32) * (dp - delta)).astype(BF)
            gq = dot(kvb[win(i), g * D : (g + 1) * D], ds, 0, 0) * SCALE
            gq = gq.T.astype(BF)
            gqb[i, :, 2 * g * D : (2 * g + 1) * D] = gq[:T]
            gqb[i, :, (2 * g + 1) * D : (2 * g + 2) * D] = gq[T:]
            acc[win(i), g * D : (g + 1) * D] += dot(ds, q2, 1, 0)
            acc[win(i), (2 + g) * D : (3 + g) * D] += dot(low, ga2, 1, 0)

        @pl.when(i == r)
        def _():
            pltpu.make_async_copy(gqb.at[i], oq.at[i], rsem.at[OQ, i]).start()

        @pl.when(i != r)
        def _():
            send(OQ, gqb.at[i], oq.at[r], base + i, i, r)

        @pl.when(has2)
        def _():
            b2s[i] = packed(i * T).astype(BF)
            send(B2, b2s.at[i], b2r.at[i], dn, i, i)

        return carry

    lax.fori_loop(0, R, backward, 0)

    def near(c, carry):
        @pl.when(mid)
        def _():
            wait_recv(B2, c, b2r.at[c])
            b1s[c] = (packed((4 + c) * T) + b2r[c].astype(F32)).astype(BF)

        @pl.when(jnp.logical_and(has_dn, jnp.logical_not(has_up)))
        def _():
            b1s[c] = packed((4 + c) * T).astype(BF)

        @pl.when(has_dn)
        def _():
            send(B1, b1s.at[c], b1r.at[c], dn, c, c)

        return carry

    lax.fori_loop(0, R, near, 0)

    def own(c, carry):
        @pl.when(has_up)
        def _():
            wait_recv(B1, c, b1r.at[c])
            kvs[c] = (packed((8 + c) * T) + b1r[c].astype(F32)).astype(BF)

        @pl.when(jnp.logical_not(has_up))
        def _():
            kvs[c] = packed((8 + c) * T).astype(BF)

        @pl.when(c == r)
        def _():
            pltpu.make_async_copy(kvs.at[c], okv.at[c], rsem.at[OKV, c]).start()

        @pl.when(c != r)
        def _():
            send(OKV, kvs.at[c], okv.at[r], base + c, c, r)

        return carry

    lax.fori_loop(0, R, own, 0)

    for o in range(1, R):
        d = peer(o)
        wait_send(KV_A, d, kchunk(8))
        wait_send(ME_A, d, meta.at[8])
        wait_send(QG_A, d, qchunk(0))
        wait_send(RW, d, rwb.at[0])
        wait_send(OQ, d, gqb.at[0])
        wait_send(OKV, d, kvs.at[0])
    for c in range(R):
        @pl.when(has_up)
        def _():
            wait_send(KV_1, c, kchunk(8 + c))
            wait_send(ME_1, c, meta.at[8 + c])

        @pl.when(mid)
        def _():
            wait_send(KV_2, c, kchunk(4 + c))
            wait_send(ME_2, c, meta.at[4 + c])

        @pl.when(has2)
        def _():
            wait_send(B2, c, b2s.at[c])

        @pl.when(has_dn)
        def _():
            wait_send(B1, c, b1s.at[c])

        wait_recv(OQ, c, oq.at[c])
        wait_recv(OKV, c, okv.at[c])


def local(n, queries, keys, values, grad_out, readout, segments, loss_mask, labels):
    tokens, heads, dim = queries.shape
    kv = keys.shape[1]

    def parts(*arrays):
        flat = [a.reshape(tokens, R, -1) for a in arrays]
        return jnp.concatenate(flat, axis=2).transpose(1, 0, 2)

    kv_in = parts(keys, values)
    qg_in = parts(queries, grad_out)
    meta = jnp.stack([segments, loss_mask, labels] + [segments] * 5).astype(F32)
    any_spec = pl.BlockSpec(memory_space=pl.ANY)
    vmem = pltpu.VMEM
    span = WINDOW + R * T
    oq, okv = pl.pallas_call(
        functools.partial(kernel, n),
        out_shape=[
            jax.ShapeDtypeStruct((R, T, 4 * D), BF),
            jax.ShapeDtypeStruct((R, T, 4 * D), BF),
        ],
        in_specs=[any_spec, any_spec, any_spec, pl.BlockSpec(memory_space=pltpu.VMEM)],
        out_specs=[any_spec, any_spec],
        scratch_shapes=[
            vmem((span, 4 * D), BF),
            vmem((R * T, 8 * D), BF),
            vmem((12, 8, T), F32),
            vmem((span, T), F32),
            vmem((4, D, D), F32),
            vmem((WINDOW + T, T), F32),
            vmem((8, WINDOW + T, 2 * T), BF),
            vmem((8, D, 2 * T), F32),
            vmem((R, R, 8, T), F32),
            vmem((span, 4 * D), F32),
            vmem((R, T, 4 * D), BF),
            vmem((R, T, 4 * D), BF),
            vmem((R, T, 4 * D), BF),
            vmem((R, T, 4 * D), BF),
            vmem((R, T, 4 * D), BF),
            vmem((R, T, 4 * D), BF),
            pltpu.SemaphoreType.DMA((12, R)),
            pltpu.SemaphoreType.DMA((12, R)),
        ],
        compiler_params=pltpu.CompilerParams(
            collective_id=0, has_side_effects=True, vmem_limit_bytes=48 * 1024 * 1024
        ),
    )(kv_in, qg_in, meta, readout)
    grad_queries = oq.transpose(1, 0, 2).reshape(tokens, heads, dim)
    both = okv.transpose(1, 0, 2)
    grad_keys = both[:, :, : 2 * D].reshape(tokens, kv, dim)
    grad_values = both[:, :, 2 * D :].reshape(tokens, kv, dim)
    return grad_queries, grad_keys, grad_values


def solution(mesh):
    tok = P(("groups", "context"), None, None)
    row = P(("groups", "context"))
    return jax.shard_map(
        functools.partial(local, mesh.shape["context"]),
        mesh=mesh,
        in_specs=(tok, tok, tok, tok, P(), row, row, row),
        out_specs=(tok, tok, tok),
        check_vma=False,
    )
```

```python
import functools

import jax
import jax.numpy as jnp
from jax import lax
from jax.experimental import pallas as pl
from jax.experimental.pallas import tpu as pltpu
from jax.sharding import PartitionSpec as P

WINDOW = 1024
SCALE = 168.0 ** (-0.5)
NEGATIVE = -1e30
MESH = pl.DeviceIdType.MESH
R = 4
T = 128
D = 128
BF = jnp.bfloat16
F32 = jnp.float32
KV_A, QG_A, ME_A, KV_1, ME_1, KV_2, ME_2, RW, B2, B1, OQ, OKV = range(12)


def dot(a, b, ca, cb):
    return lax.dot_general(a, b, (((ca,), (cb,)), ((), ())), preferred_element_type=F32)


def kernel(
    n, kv_in, qg_in, me_in, ro_ref, oq, okv,
    kvb, qgb, meta, segc, rob, bias, pb, ob, rwb, acc, gqb, b2s, b2r, b1s, b1r, kvs,
    ssem, rsem,
):
    planes = n // R
    me = lax.axis_index("context")
    r = lax.rem(me, R)
    p = lax.div(me, R)
    base = p * R
    has_dn = p >= 1
    has_up = p < planes - 1
    has2 = p >= 2
    mid = jnp.logical_and(has_dn, has_up)
    up = me + R
    dn = me - R

    def send(k, src, dst, to, s, d):
        pltpu.make_async_remote_copy(
            src_ref=src, dst_ref=dst, send_sem=ssem.at[k, s], recv_sem=rsem.at[k, d],
            device_id={"context": to}, device_id_type=MESH,
        ).start()

    def wait_recv(k, c, ref):
        pltpu.make_async_copy(ref, ref, rsem.at[k, c]).wait()

    def wait_send(k, c, ref):
        pltpu.make_async_copy(ref, ref, ssem.at[k, c]).wait()

    def peer(o):
        return lax.rem(r + o, R)

    def rows(start):
        return pl.ds(pl.multiple_of(start, T), T)

    def kchunk(c):
        return kvb.at[rows(c * T)]

    def qchunk(c):
        return qgb.at[rows(c * T)]

    barrier = pltpu.get_barrier_semaphore()
    for o in range(1, R):
        pl.semaphore_signal(barrier, inc=1, device_id={"context": base + peer(o)}, device_id_type=MESH)

    @pl.when(has_dn)
    def _():
        pl.semaphore_signal(barrier, inc=1, device_id={"context": dn}, device_id_type=MESH)

    @pl.when(has_up)
    def _():
        pl.semaphore_signal(barrier, inc=1, device_id={"context": up}, device_id_type=MESH)

    pltpu.make_async_copy(kv_in.at[r], kchunk(8 + r), rsem.at[KV_A, r]).start()
    pltpu.make_async_copy(me_in, meta.at[8 + r], rsem.at[ME_A, r]).start()
    pltpu.make_async_copy(qg_in.at[r], qchunk(r), rsem.at[QG_A, r]).start()
    pl.semaphore_wait(barrier, R - 1 + has_dn.astype(jnp.int32) + has_up.astype(jnp.int32))

    for o in range(1, R):
        d = peer(o)
        send(KV_A, kv_in.at[d], kchunk(8 + r), base + d, d, r)
        send(ME_A, me_in, meta.at[8 + r], base + d, d, r)
    for k in range(R):
        c = lax.rem(lax.div(r, 2) + k // 2, 2) * 2 + lax.rem(r + k, 2)
        wait_recv(KV_A, c, kchunk(8 + c))
        wait_recv(ME_A, c, meta.at[8 + c])

        @pl.when(has_up)
        def _():
            send(KV_1, kchunk(8 + c), kchunk(4 + c), up, c, c)
            send(ME_1, meta.at[8 + c], meta.at[4 + c], up, c, c)

    for o in range(1, R):
        d = peer(o)
        send(QG_A, qg_in.at[d], qchunk(r), base + d, d, r)

    @pl.when(jnp.logical_not(has_dn))
    def _():
        kvb[4 * T : 8 * T] = jnp.zeros((4 * T, 4 * D), BF)
        meta[4:8] = jnp.full((4, 8, T), -1.0, F32)

    @pl.when(jnp.logical_not(has2))
    def _():
        kvb[0 : 4 * T] = jnp.zeros((4 * T, 4 * D), BF)
        meta[0:4] = jnp.full((4, 8, T), -1.0, F32)

    acc[...] = jnp.zeros_like(acc)
    for h in range(4):
        rob[h] = jnp.broadcast_to(ro_ref[pl.ds(4 * r + h, 1), :], (D, D)).T

    for c in range(R - 1, -1, -1):
        @pl.when(has_dn)
        def _():
            wait_recv(KV_1, c, kchunk(4 + c))
            wait_recv(ME_1, c, meta.at[4 + c])

        @pl.when(mid)
        def _():
            send(KV_2, kchunk(4 + c), kchunk(c), up, c, c)
            send(ME_2, meta.at[4 + c], meta.at[c], up, c, c)

    for c in range(R):
        wait_recv(QG_A, c, qchunk(c))

    def seg_column(c):
        segc[rows(c * T)] = jnp.broadcast_to(meta[c, 0:1, :], (T, T)).T

    def seg_body(c, carry):
        seg_column(c + 4)
        return carry

    lax.fori_loop(0, 8, seg_body, 0)

    def win(i):
        return pl.ds(pl.multiple_of(i * T, T), WINDOW + T)

    def two(ref, i, g, at):
        lane = at + 2 * g * D
        return jnp.concatenate(
            [ref[rows(i * T), lane : lane + D], ref[rows(i * T), lane + D : lane + 2 * D]], axis=0
        )

    def forward(step, carry):
        i = R - 1 - step

        @pl.when(has2)
        def _():
            wait_recv(KV_2, i, kchunk(i))
            wait_recv(ME_2, i, meta.at[i])

        seg_column(i)
        seg_q = meta[8 + i, 0:1, :]
        for j in range(9):
            ok = segc[rows((i + j) * T)] == seg_q
            if j in (0, 8):
                kk = lax.broadcasted_iota(jnp.int32, (T, T), 0)
                tq = lax.broadcasted_iota(jnp.int32, (T, T), 1)
                ok = jnp.logical_and(ok, kk > tq if j == 0 else kk <= tq)
            bias[j * T : (j + 1) * T] = jnp.where(ok, 0.0, NEGATIVE)
        total = jnp.zeros((1, T), F32)
        for g in range(2):
            q2 = two(qgb, i, g, 0)
            s = dot(kvb[win(i), g * D : (g + 1) * D], q2, 1, 1) * SCALE
            b = bias[...]
            s = s + jnp.concatenate([b, b], axis=1)
            e = jnp.exp(s - jnp.max(s, axis=0, keepdims=True))
            low = (e * (1.0 / jnp.sum(e, axis=0, keepdims=True))).astype(BF)
            pb[2 * i + g] = low
            o = dot(kvb[win(i), (2 + g) * D : (3 + g) * D], low, 0, 0)
            ob[2 * i + g] = o
            w = o[:, :T] * rob[2 * g] + o[:, T:] * rob[2 * g + 1]
            total = total + jnp.sum(w, axis=0, keepdims=True)
        rwb[r, i] = jnp.broadcast_to(total, (8, T))
        return carry

    lax.fori_loop(0, R, forward, 0)

    for o in range(1, R):
        send(RW, rwb.at[r], rwb.at[r], base + peer(o), peer(o), r)
    for o in range(1, R):
        wait_recv(RW, peer(o), rwb.at[peer(o)])

    def packed(start):
        return jnp.concatenate(
            [acc[rows(start), : 2 * D] * SCALE, acc[rows(start), 2 * D :]], axis=1
        )

    def backward(i, carry):
        reward = jnp.sum(rwb[:, i, 0:1, :], axis=0)
        live = meta[8 + i, 1:2, :]
        pg = live * (jax.nn.sigmoid(reward) - meta[8 + i, 2:3, :])
        for g in range(2):
            q2 = two(qgb, i, g, 0)
            go = two(qgb, i, g, 4 * D).astype(F32).T
            ga_t = jnp.concatenate(
                [
                    live * go[:, :T] + pg * rob[2 * g],
                    live * go[:, T:] + pg * rob[2 * g + 1],
                ],
                axis=1,
            ).astype(BF)
            ga_f = ga_t.astype(F32)
            ga2 = ga_f.T.astype(BF)
            delta = jnp.sum(ga_f * ob[2 * i + g], axis=0, keepdims=True)
            low = pb[2 * i + g]
            dp = dot(kvb[win(i), (2 + g) * D : (3 + g) * D], ga_t, 1, 0)
            ds = (low.astype(F32) * (dp - delta)).astype(BF)
            gq = dot(kvb[win(i), g * D : (g + 1) * D], ds, 0, 0) * SCALE
            gq = gq.T.astype(BF)
            gqb[i, :, 2 * g * D : (2 * g + 1) * D] = gq[:T]
            gqb[i, :, (2 * g + 1) * D : (2 * g + 2) * D] = gq[T:]
            acc[win(i), g * D : (g + 1) * D] += dot(ds, q2, 1, 0)
            acc[win(i), (2 + g) * D : (3 + g) * D] += dot(low, ga2, 1, 0)

        @pl.when(i == r)
        def _():
            pltpu.make_async_copy(gqb.at[i], oq.at[i], rsem.at[OQ, i]).start()

        @pl.when(i != r)
        def _():
            send(OQ, gqb.at[i], oq.at[r], base + i, i, r)

        @pl.when(has2)
        def _():
            b2s[i] = packed(i * T).astype(BF)
            send(B2, b2s.at[i], b2r.at[i], dn, i, i)

        return carry

    lax.fori_loop(0, R, backward, 0)

    def near(c, carry):
        @pl.when(mid)
        def _():
            wait_recv(B2, c, b2r.at[c])
            b1s[c] = (packed((4 + c) * T) + b2r[c].astype(F32)).astype(BF)

        @pl.when(jnp.logical_and(has_dn, jnp.logical_not(has_up)))
        def _():
            b1s[c] = packed((4 + c) * T).astype(BF)

        @pl.when(has_dn)
        def _():
            send(B1, b1s.at[c], b1r.at[c], dn, c, c)

        return carry

    lax.fori_loop(0, R, near, 0)

    def own(c, carry):
        @pl.when(has_up)
        def _():
            wait_recv(B1, c, b1r.at[c])
            kvs[c] = (packed((8 + c) * T) + b1r[c].astype(F32)).astype(BF)

        @pl.when(jnp.logical_not(has_up))
        def _():
            kvs[c] = packed((8 + c) * T).astype(BF)

        @pl.when(c == r)
        def _():
            pltpu.make_async_copy(kvs.at[c], okv.at[c], rsem.at[OKV, c]).start()

        @pl.when(c != r)
        def _():
            send(OKV, kvs.at[c], okv.at[r], base + c, c, r)

        return carry

    lax.fori_loop(0, R, own, 0)

    for o in range(1, R):
        d = peer(o)
        wait_send(KV_A, d, kchunk(8))
        wait_send(ME_A, d, meta.at[8])
        wait_send(QG_A, d, qchunk(0))
        wait_send(RW, d, rwb.at[0])
        wait_send(OQ, d, gqb.at[0])
        wait_send(OKV, d, kvs.at[0])
    for c in range(R):
        @pl.when(has_up)
        def _():
            wait_send(KV_1, c, kchunk(8 + c))
            wait_send(ME_1, c, meta.at[8 + c])

        @pl.when(mid)
        def _():
            wait_send(KV_2, c, kchunk(4 + c))
            wait_send(ME_2, c, meta.at[4 + c])

        @pl.when(has2)
        def _():
            wait_send(B2, c, b2s.at[c])

        @pl.when(has_dn)
        def _():
            wait_send(B1, c, b1s.at[c])

        wait_recv(OQ, c, oq.at[c])
        wait_recv(OKV, c, okv.at[c])


def local(n, queries, keys, values, grad_out, readout, segments, loss_mask, labels):
    tokens, heads, dim = queries.shape
    kv = keys.shape[1]

    def parts(*arrays):
        flat = [a.reshape(tokens, R, -1) for a in arrays]
        return jnp.concatenate(flat, axis=2).transpose(1, 0, 2)

    kv_in = parts(keys, values)
    qg_in = parts(queries, grad_out)
    meta = jnp.stack([segments, loss_mask, labels] + [segments] * 5).astype(F32)
    any_spec = pl.BlockSpec(memory_space=pl.ANY)
    vmem = pltpu.VMEM
    span = WINDOW + R * T
    oq, okv = pl.pallas_call(
        functools.partial(kernel, n),
        out_shape=[
            jax.ShapeDtypeStruct((R, T, 4 * D), BF),
            jax.ShapeDtypeStruct((R, T, 4 * D), BF),
        ],
        in_specs=[any_spec, any_spec, any_spec, pl.BlockSpec(memory_space=pltpu.VMEM)],
        out_specs=[any_spec, any_spec],
        scratch_shapes=[
            vmem((span, 4 * D), BF),
            vmem((R * T, 8 * D), BF),
            vmem((12, 8, T), F32),
            vmem((span, T), F32),
            vmem((4, D, D), F32),
            vmem((WINDOW + T, T), F32),
            vmem((8, WINDOW + T, 2 * T), BF),
            vmem((8, D, 2 * T), F32),
            vmem((R, R, 8, T), F32),
            vmem((span, 4 * D), F32),
            vmem((R, T, 4 * D), BF),
            vmem((R, T, 4 * D), BF),
            vmem((R, T, 4 * D), BF),
            vmem((R, T, 4 * D), BF),
            vmem((R, T, 4 * D), BF),
            vmem((R, T, 4 * D), BF),
            pltpu.SemaphoreType.DMA((12, R)),
            pltpu.SemaphoreType.DMA((12, R)),
        ],
        compiler_params=pltpu.CompilerParams(
            collective_id=0, has_side_effects=True, vmem_limit_bytes=48 * 1024 * 1024
        ),
    )(kv_in, qg_in, meta, readout)
    grad_queries = oq.transpose(1, 0, 2).reshape(tokens, heads, dim)
    both = okv.transpose(1, 0, 2)
    grad_keys = both[:, :, : 2 * D].reshape(tokens, kv, dim)
    grad_values = both[:, :, 2 * D :].reshape(tokens, kv, dim)
    return grad_queries, grad_keys, grad_values


def solution(mesh):
    tok = P(("groups", "context"), None, None)
    row = P(("groups", "context"))
    return jax.shard_map(
        functools.partial(local, mesh.shape["context"]),
        mesh=mesh,
        in_specs=(tok, tok, tok, tok, P(), row, row, row),
        out_specs=(tok, tok, tok),
        check_vma=False,
    )
```

```python
import functools

import jax
import jax.numpy as jnp
from jax import lax
from jax.experimental import pallas as pl
from jax.experimental.pallas import tpu as pltpu
from jax.sharding import PartitionSpec as P

WINDOW = 1024
SCALE = 168.0 ** (-0.5)
NEGATIVE = -1e30
LOG2E = 1.4426950408889634
MESH = pl.DeviceIdType.MESH
R = 4
T = 128
D = 128
BF = jnp.bfloat16
F32 = jnp.float32
KV_A, QG_A, ME_A, KV_1, ME_1, KV_2, ME_2, RW, B2, B1, OQ, OKV = range(12)


def dot(a, b, ca, cb):
    return lax.dot_general(a, b, (((ca,), (cb,)), ((), ())), preferred_element_type=F32)


def kernel(
    n, kv_in, qg_in, seg_ref, live_ref, lab_ref, ro_ref, oq, okv,
    kvb, qgb, meta, segc, rob, bias, pb, ob, rwb, acc, gqb, b2s, b2r, b1s, b1r, kvs,
    me_in, kvt, sb, dsb, inv,
    ssem, rsem,
):
    planes = n // R
    me = lax.axis_index("context")
    r = lax.rem(me, R)
    p = lax.div(me, R)
    base = p * R
    has_dn = p >= 1
    has_up = p < planes - 1
    has2 = p >= 2
    mid = jnp.logical_and(has_dn, has_up)
    up = me + R
    dn = me - R

    def send(k, src, dst, to, s, d):
        pltpu.make_async_remote_copy(
            src_ref=src, dst_ref=dst, send_sem=ssem.at[k, s], recv_sem=rsem.at[k, d],
            device_id={"context": to}, device_id_type=MESH,
        ).start()

    def wait_recv(k, c, ref):
        pltpu.make_async_copy(ref, ref, rsem.at[k, c]).wait()

    def wait_send(k, c, ref):
        pltpu.make_async_copy(ref, ref, ssem.at[k, c]).wait()

    def peer(o):
        return lax.rem(r + o, R)

    def rows(start):
        return pl.ds(pl.multiple_of(start, T), T)

    def kchunk(c):
        return kvb.at[rows(c * T)]

    def qchunk(c):
        return qgb.at[rows(c * T)]

    barrier = pltpu.get_barrier_semaphore()
    for o in range(1, R):
        pl.semaphore_signal(barrier, inc=1, device_id={"context": base + peer(o)}, device_id_type=MESH)

    @pl.when(has_dn)
    def _():
        pl.semaphore_signal(barrier, inc=1, device_id={"context": dn}, device_id_type=MESH)

    @pl.when(has_up)
    def _():
        pl.semaphore_signal(barrier, inc=1, device_id={"context": up}, device_id_type=MESH)

    me_in[...] = jnp.concatenate(
        [seg_ref[...], live_ref[...], lab_ref[...], jnp.zeros((5, T), jnp.int32)], axis=0
    ).astype(F32)
    pltpu.make_async_copy(kv_in.at[r], kchunk(8 + r), rsem.at[KV_A, r]).start()
    pltpu.make_async_copy(me_in, meta.at[8 + r], rsem.at[ME_A, r]).start()
    pltpu.make_async_copy(qg_in.at[r], qchunk(r), rsem.at[QG_A, r]).start()
    pl.semaphore_wait(barrier, R - 1 + has_dn.astype(jnp.int32) + has_up.astype(jnp.int32))

    for o in range(1, R):
        d = peer(o)
        send(KV_A, kv_in.at[d], kchunk(8 + r), base + d, d, r)
        send(ME_A, me_in, meta.at[8 + r], base + d, d, r)
    for k in range(R):
        c = lax.rem(lax.div(r, 2) + k // 2, 2) * 2 + lax.rem(r + k, 2)
        wait_recv(KV_A, c, kchunk(8 + c))
        wait_recv(ME_A, c, meta.at[8 + c])

        @pl.when(has_up)
        def _():
            send(KV_1, kchunk(8 + c), kchunk(4 + c), up, c, c)
            send(ME_1, meta.at[8 + c], meta.at[4 + c], up, c, c)

    for o in range(1, R):
        d = peer(o)
        send(QG_A, qg_in.at[d], qchunk(r), base + d, d, r)

    @pl.when(jnp.logical_not(has_dn))
    def _():
        kvb[4 * T : 8 * T] = jnp.zeros((4 * T, 4 * D), BF)
        meta[4:8] = jnp.full((4, 8, T), -1.0, F32)

    @pl.when(jnp.logical_not(has2))
    def _():
        kvb[0 : 4 * T] = jnp.zeros((4 * T, 4 * D), BF)
        meta[0:4] = jnp.full((4, 8, T), -1.0, F32)

    acc[...] = jnp.zeros_like(acc)
    for h in range(4):
        rob[h] = jnp.broadcast_to(ro_ref[pl.ds(4 * r + h, 1), :], (D, D)).T

    for c in range(R - 1, -1, -1):
        @pl.when(has_dn)
        def _():
            wait_recv(KV_1, c, kchunk(4 + c))
            wait_recv(ME_1, c, meta.at[4 + c])

        @pl.when(mid)
        def _():
            send(KV_2, kchunk(4 + c), kchunk(c), up, c, c)
            send(ME_2, meta.at[4 + c], meta.at[c], up, c, c)

    for c in range(R):
        wait_recv(QG_A, c, qchunk(c))

    def seg_column(c):
        segc[rows(c * T)] = jnp.broadcast_to(meta[c, 0:1, :], (T, T)).T
        kvt[:, rows(c * T)] = kvb[rows(c * T)].T

    def seg_body(c, carry):
        seg_column(c + 4)
        return carry

    lax.fori_loop(0, 8, seg_body, 0)

    def win(i):
        return pl.ds(pl.multiple_of(i * T, T), WINDOW + T)

    def two(ref, i, g, at):
        lane = at + 2 * g * D
        return jnp.concatenate(
            [ref[rows(i * T), lane : lane + D], ref[rows(i * T), lane + D : lane + 2 * D]], axis=0
        )

    def forward(step, carry):
        i = R - 1 - step

        @pl.when(has2)
        def _():
            wait_recv(KV_2, i, kchunk(i))
            wait_recv(ME_2, i, meta.at[i])

        seg_column(i)
        seg_q = meta[8 + i, 0:1, :]
        for j in range(9):
            ok = segc[rows((i + j) * T)] == seg_q
            if j in (0, 8):
                kk = lax.broadcasted_iota(jnp.int32, (T, T), 0)
                tq = lax.broadcasted_iota(jnp.int32, (T, T), 1)
                ok = jnp.logical_and(ok, kk > tq if j == 0 else kk <= tq)
            bias[j * T : (j + 1) * T] = jnp.where(ok, 0.0, NEGATIVE)
        total = jnp.zeros((1, T), F32)
        for g in range(2):
            q2 = two(qgb, i, g, 0)
            top = None
            for j in range(9):
                at = slice(j * T, (j + 1) * T)
                raw = dot(kvb[rows((i + j) * T), g * D : (g + 1) * D], q2, 1, 1)
                b = bias[at]
                x = raw * (SCALE * LOG2E) + jnp.concatenate([b, b], axis=1)
                sb[g, at] = x
                m = jnp.max(x.reshape(T // 8, 8, 2 * T), axis=0)
                top = m if top is None else jnp.maximum(top, m)
            top = jnp.max(top, axis=0, keepdims=True)
            total_e = None
            for j in range(9):
                at = slice(j * T, (j + 1) * T)
                e = jnp.exp2(sb[g, at] - top)
                pb[2 * i + g, at] = e.astype(BF)
                m = jnp.sum(e.reshape(T // 8, 8, 2 * T), axis=0)
                total_e = m if total_e is None else total_e + m
            part = 1.0 / jnp.sum(total_e, axis=0, keepdims=True)
            inv[2 * i + g] = jnp.broadcast_to(part, (8, 2 * T))
            vt = kvt[(2 + g) * D : (3 + g) * D, win(i)]
            o = dot(vt, pb[2 * i + g], 1, 0) * part
            ob[2 * i + g] = o
            w = o[:, :T] * rob[2 * g] + o[:, T:] * rob[2 * g + 1]
            total = total + jnp.sum(w, axis=0, keepdims=True)
        rwb[r, i] = jnp.broadcast_to(total, (8, T))
        return carry

    lax.fori_loop(0, R, forward, 0)

    for o in range(1, R):
        send(RW, rwb.at[r], rwb.at[r], base + peer(o), peer(o), r)
    for o in range(1, R):
        wait_recv(RW, peer(o), rwb.at[peer(o)])

    def packed(start):
        return jnp.concatenate(
            [acc[rows(start), : 2 * D] * SCALE, acc[rows(start), 2 * D :]], axis=1
        )

    def backward(i, carry):
        reward = jnp.sum(rwb[:, i, 0:1, :], axis=0)
        live = meta[8 + i, 1:2, :]
        pg = live * (jax.nn.sigmoid(reward) - meta[8 + i, 2:3, :])
        for g in range(2):
            q2 = two(qgb, i, g, 0)
            go = two(qgb, i, g, 4 * D).astype(F32).T
            ga_t = jnp.concatenate(
                [
                    live * go[:, :T] + pg * rob[2 * g],
                    live * go[:, T:] + pg * rob[2 * g + 1],
                ],
                axis=1,
            ).astype(BF)
            ga_f = ga_t.astype(F32)
            part = inv[2 * i + g, 0:1, :]
            delta = jnp.sum(ga_f * ob[2 * i + g], axis=0, keepdims=True) * part
            ga2 = (ga_f * part).T.astype(BF)
            for j in range(9):
                at = slice(j * T, (j + 1) * T)
                here = rows((i + j) * T)
                low = pb[2 * i + g, at]
                dp = dot(kvb[here, (2 + g) * D : (3 + g) * D], ga_t, 1, 0)
                ds = (low.astype(F32) * (dp * part - delta)).astype(BF)
                dsb[g, at] = ds
                acc[here, g * D : (g + 1) * D] += dot(ds, q2, 1, 0)
                acc[here, (2 + g) * D : (3 + g) * D] += dot(low, ga2, 1, 0)
            gq = dot(kvt[g * D : (g + 1) * D, win(i)], dsb[g], 1, 0) * SCALE
            gq = gq.T.astype(BF)
            gqb[i, :, 2 * g * D : (2 * g + 1) * D] = gq[:T]
            gqb[i, :, (2 * g + 1) * D : (2 * g + 2) * D] = gq[T:]

        @pl.when(i == r)
        def _():
            pltpu.make_async_copy(gqb.at[i], oq.at[i], rsem.at[OQ, i]).start()

        @pl.when(i != r)
        def _():
            send(OQ, gqb.at[i], oq.at[r], base + i, i, r)

        @pl.when(has2)
        def _():
            b2s[i] = packed(i * T).astype(BF)
            send(B2, b2s.at[i], b2r.at[i], dn, i, i)

        return carry

    lax.fori_loop(0, R, backward, 0)

    def near(c, carry):
        @pl.when(mid)
        def _():
            wait_recv(B2, c, b2r.at[c])
            b1s[c] = (packed((4 + c) * T) + b2r[c].astype(F32)).astype(BF)

        @pl.when(jnp.logical_and(has_dn, jnp.logical_not(has_up)))
        def _():
            b1s[c] = packed((4 + c) * T).astype(BF)

        @pl.when(has_dn)
        def _():
            send(B1, b1s.at[c], b1r.at[c], dn, c, c)

        return carry

    lax.fori_loop(0, R, near, 0)

    def own(c, carry):
        @pl.when(has_up)
        def _():
            wait_recv(B1, c, b1r.at[c])
            kvs[c] = (packed((8 + c) * T) + b1r[c].astype(F32)).astype(BF)

        @pl.when(jnp.logical_not(has_up))
        def _():
            kvs[c] = packed((8 + c) * T).astype(BF)

        @pl.when(c == r)
        def _():
            pltpu.make_async_copy(kvs.at[c], okv.at[c], rsem.at[OKV, c]).start()

        @pl.when(c != r)
        def _():
            send(OKV, kvs.at[c], okv.at[r], base + c, c, r)

        return carry

    lax.fori_loop(0, R, own, 0)

    for o in range(1, R):
        d = peer(o)
        wait_send(KV_A, d, kchunk(8))
        wait_send(ME_A, d, meta.at[8])
        wait_send(QG_A, d, qchunk(0))
        wait_send(RW, d, rwb.at[0])
        wait_send(OQ, d, gqb.at[0])
        wait_send(OKV, d, kvs.at[0])
    for c in range(R):
        @pl.when(has_up)
        def _():
            wait_send(KV_1, c, kchunk(8 + c))
            wait_send(ME_1, c, meta.at[8 + c])

        @pl.when(mid)
        def _():
            wait_send(KV_2, c, kchunk(4 + c))
            wait_send(ME_2, c, meta.at[4 + c])

        @pl.when(has2)
        def _():
            wait_send(B2, c, b2s.at[c])

        @pl.when(has_dn)
        def _():
            wait_send(B1, c, b1s.at[c])

        wait_recv(OQ, c, oq.at[c])
        wait_recv(OKV, c, okv.at[c])


def local(n, queries, keys, values, grad_out, readout, segments, loss_mask, labels):
    tokens, heads, dim = queries.shape
    kv = keys.shape[1]

    def parts(*arrays):
        flat = [a.reshape(tokens, R, -1) for a in arrays]
        return jnp.concatenate(flat, axis=2).transpose(1, 0, 2)

    kv_in = parts(keys, values)
    qg_in = parts(queries, grad_out)
    rows3 = [x.reshape(1, tokens) for x in (segments, loss_mask, labels)]
    any_spec = pl.BlockSpec(memory_space=pl.ANY)
    vmem = pltpu.VMEM
    span = WINDOW + R * T
    oq, okv = pl.pallas_call(
        functools.partial(kernel, n),
        out_shape=[
            jax.ShapeDtypeStruct((R, T, 4 * D), BF),
            jax.ShapeDtypeStruct((R, T, 4 * D), BF),
        ],
        in_specs=[any_spec, any_spec] + [pl.BlockSpec(memory_space=pltpu.VMEM)] * 4,
        out_specs=[any_spec, any_spec],
        scratch_shapes=[
            vmem((span, 4 * D), BF),
            vmem((R * T, 8 * D), BF),
            vmem((12, 8, T), F32),
            vmem((span, T), F32),
            vmem((4, D, D), F32),
            vmem((WINDOW + T, T), F32),
            vmem((8, WINDOW + T, 2 * T), BF),
            vmem((8, D, 2 * T), F32),
            vmem((R, R, 8, T), F32),
            vmem((span, 4 * D), F32),
            vmem((R, T, 4 * D), BF),
            vmem((R, T, 4 * D), BF),
            vmem((R, T, 4 * D), BF),
            vmem((R, T, 4 * D), BF),
            vmem((R, T, 4 * D), BF),
            vmem((R, T, 4 * D), BF),
            vmem((8, T), F32),
            vmem((4 * D, span), BF),
            vmem((2, WINDOW + T, 2 * T), F32),
            vmem((2, WINDOW + T, 2 * T), BF),
            vmem((8, 8, 2 * T), F32),
            pltpu.SemaphoreType.DMA((12, R)),
            pltpu.SemaphoreType.DMA((12, R)),
        ],
        compiler_params=pltpu.CompilerParams(
            collective_id=0, has_side_effects=True, vmem_limit_bytes=48 * 1024 * 1024
        ),
    )(kv_in, qg_in, *rows3, readout)
    grad_queries = oq.transpose(1, 0, 2).reshape(tokens, heads, dim)
    both = okv.transpose(1, 0, 2)
    grad_keys = both[:, :, : 2 * D].reshape(tokens, kv, dim)
    grad_values = both[:, :, 2 * D :].reshape(tokens, kv, dim)
    return grad_queries, grad_keys, grad_values


def solution(mesh):
    tok = P(("groups", "context"), None, None)
    row = P(("groups", "context"))
    return jax.shard_map(
        functools.partial(local, mesh.shape["context"]),
        mesh=mesh,
        in_specs=(tok, tok, tok, tok, P(), row, row, row),
        out_specs=(tok, tok, tok),
        check_vma=False,
    )
```

```python
import functools

import jax
import jax.numpy as jnp
from jax import lax
from jax.experimental import pallas as pl
from jax.experimental.pallas import tpu as pltpu
from jax.sharding import PartitionSpec as P

WINDOW = 1024
SCALE = 168.0 ** (-0.5)
NEGATIVE = -1e30
LOG2E = 1.4426950408889634
MESH = pl.DeviceIdType.MESH
R = 4
T = 128
D = 128
BF = jnp.bfloat16
F32 = jnp.float32
KV_A, QG_A, ME_A, KV_1, ME_1, KV_2, ME_2, RW, B2, B1, OQ, OKV = range(12)


def dot(a, b, ca, cb):
    return lax.dot_general(a, b, (((ca,), (cb,)), ((), ())), preferred_element_type=F32)


def kernel(
    n, kv_in, qg_in, seg_ref, live_ref, lab_ref, ro_ref, oq, okv,
    kvb, qgb, meta, segc, rob, pb, ob, rwb, acc, gqb, b2s, b2r, b1s, b1r, kvs,
    me_in, kvt, sb, dsb, inv,
    ssem, rsem,
):
    planes = n // R
    me = lax.axis_index("context")
    r = lax.rem(me, R)
    p = lax.div(me, R)
    base = p * R
    has_dn = p >= 1
    has_up = p < planes - 1
    has2 = p >= 2
    mid = jnp.logical_and(has_dn, has_up)
    up = me + R
    dn = me - R

    def send(k, src, dst, to, s, d):
        pltpu.make_async_remote_copy(
            src_ref=src, dst_ref=dst, send_sem=ssem.at[k, s], recv_sem=rsem.at[k, d],
            device_id={"context": to}, device_id_type=MESH,
        ).start()

    def wait_recv(k, c, ref):
        pltpu.make_async_copy(ref, ref, rsem.at[k, c]).wait()

    def wait_send(k, c, ref):
        pltpu.make_async_copy(ref, ref, ssem.at[k, c]).wait()

    def peer(o):
        return lax.rem(r + o, R)

    def rows(start):
        return pl.ds(pl.multiple_of(start, T), T)

    def kchunk(c):
        return kvb.at[rows(c * T)]

    def qchunk(c):
        return qgb.at[rows(c * T)]

    barrier = pltpu.get_barrier_semaphore()
    for o in range(1, R):
        pl.semaphore_signal(barrier, inc=1, device_id={"context": base + peer(o)}, device_id_type=MESH)

    @pl.when(has_dn)
    def _():
        pl.semaphore_signal(barrier, inc=1, device_id={"context": dn}, device_id_type=MESH)

    @pl.when(has_up)
    def _():
        pl.semaphore_signal(barrier, inc=1, device_id={"context": up}, device_id_type=MESH)

    me_in[...] = jnp.concatenate(
        [seg_ref[...], live_ref[...], lab_ref[...], jnp.zeros((5, T), jnp.int32)], axis=0
    ).astype(F32)
    pltpu.make_async_copy(kv_in.at[r], kchunk(8 + r), rsem.at[KV_A, r]).start()
    pltpu.make_async_copy(me_in, meta.at[8 + r], rsem.at[ME_A, r]).start()
    pltpu.make_async_copy(qg_in.at[r], qchunk(r), rsem.at[QG_A, r]).start()
    pl.semaphore_wait(barrier, R - 1 + has_dn.astype(jnp.int32) + has_up.astype(jnp.int32))

    for o in range(1, R):
        d = peer(o)
        send(KV_A, kv_in.at[d], kchunk(8 + r), base + d, d, r)
        send(ME_A, me_in, meta.at[8 + r], base + d, d, r)
    for k in range(R):
        c = lax.rem(5 - k + 2 * lax.div(r, 2), R)
        wait_recv(KV_A, c, kchunk(8 + c))
        wait_recv(ME_A, c, meta.at[8 + c])

        @pl.when(has_up)
        def _():
            send(KV_1, kchunk(8 + c), kchunk(4 + c), up, c, c)
            send(ME_1, meta.at[8 + c], meta.at[4 + c], up, c, c)

    for o in range(1, R):
        d = peer(o)
        send(QG_A, qg_in.at[d], qchunk(r), base + d, d, r)

    @pl.when(jnp.logical_not(has_dn))
    def _():
        kvb[4 * T : 8 * T] = jnp.zeros((4 * T, 4 * D), BF)
        meta[4:8] = jnp.full((4, 8, T), -1.0, F32)

    @pl.when(jnp.logical_not(has2))
    def _():
        kvb[0 : 4 * T] = jnp.zeros((4 * T, 4 * D), BF)
        meta[0:4] = jnp.full((4, 8, T), -1.0, F32)

    acc[...] = jnp.zeros_like(acc)
    for h in range(4):
        rob[h] = jnp.broadcast_to(ro_ref[pl.ds(4 * r + h, 1), :], (D, D)).T

    for c in range(R - 1, -1, -1):
        @pl.when(has_dn)
        def _():
            wait_recv(KV_1, c, kchunk(4 + c))
            wait_recv(ME_1, c, meta.at[4 + c])

        @pl.when(mid)
        def _():
            send(KV_2, kchunk(4 + c), kchunk(c), up, c, c)
            send(ME_2, meta.at[4 + c], meta.at[c], up, c, c)

    for c in range(R):
        wait_recv(QG_A, c, qchunk(c))

    def seg_column(c):
        segc[rows(c * T)] = jnp.broadcast_to(meta[c, 0:1, :], (T, T)).T
        kvt[:, rows(c * T)] = kvb[rows(c * T)].T

    def seg_body(c, carry):
        seg_column(c + 4)
        return carry

    lax.fori_loop(0, 8, seg_body, 0)

    def win(i):
        return pl.ds(pl.multiple_of(i * T, T), WINDOW + T)

    def two(ref, i, g, at):
        lane = at + 2 * g * D
        return jnp.concatenate(
            [ref[rows(i * T), lane : lane + D], ref[rows(i * T), lane + D : lane + 2 * D]], axis=0
        )

    def forward(step, carry):
        i = R - 1 - step

        seg_q = meta[8 + i, 0:1, :]
        q2s = [two(qgb, i, g, 0) for g in range(2)]

        def scores(j, tops):
            at = slice(j * T, (j + 1) * T)
            ok = segc[rows((i + j) * T)] == seg_q
            if j in (0, 8):
                kk = lax.broadcasted_iota(jnp.int32, (T, T), 0)
                tq = lax.broadcasted_iota(jnp.int32, (T, T), 1)
                ok = jnp.logical_and(ok, kk > tq if j == 0 else kk <= tq)
            b = jnp.where(ok, 0.0, NEGATIVE)
            b = jnp.concatenate([b, b], axis=1)
            new = []
            for g in range(2):
                raw = dot(kvb[rows((i + j) * T), g * D : (g + 1) * D], q2s[g], 1, 1)
                x = raw * (SCALE * LOG2E) + b
                sb[g, at] = x
                m = jnp.max(x.reshape(T // 8, 8, 2 * T), axis=0)
                new.append(jnp.maximum(tops[g], m))
            return new

        tops = [jnp.full((8, 2 * T), 2 * NEGATIVE, F32)] * 2
        for j in range(1, 9):
            tops = scores(j, tops)

        @pl.when(has2)
        def _():
            wait_recv(KV_2, i, kchunk(i))
            wait_recv(ME_2, i, meta.at[i])

        seg_column(i)
        tops = scores(0, tops)
        total = jnp.zeros((1, T), F32)
        for g in range(2):
            top = tops[g]
            top = jnp.max(top, axis=0, keepdims=True)
            total_e = None
            for j in range(9):
                at = slice(j * T, (j + 1) * T)
                e = jnp.exp2(sb[g, at] - top)
                pb[2 * i + g, at] = e.astype(BF)
                m = jnp.sum(e.reshape(T // 8, 8, 2 * T), axis=0)
                total_e = m if total_e is None else total_e + m
            part = 1.0 / jnp.sum(total_e, axis=0, keepdims=True)
            inv[2 * i + g] = jnp.broadcast_to(part, (8, 2 * T))
            vt = kvt[(2 + g) * D : (3 + g) * D, win(i)]
            o = dot(vt, pb[2 * i + g], 1, 0) * part
            ob[2 * i + g] = o
            w = o[:, :T] * rob[2 * g] + o[:, T:] * rob[2 * g + 1]
            total = total + jnp.sum(w, axis=0, keepdims=True)
        rwb[r, i] = jnp.broadcast_to(total, (8, T))
        return carry

    lax.fori_loop(0, R, forward, 0)

    for o in range(1, R):
        send(RW, rwb.at[r], rwb.at[r], base + peer(o), peer(o), r)
    for o in range(1, R):
        wait_recv(RW, peer(o), rwb.at[peer(o)])

    def packed(start):
        return jnp.concatenate(
            [acc[rows(start), : 2 * D] * SCALE, acc[rows(start), 2 * D :]], axis=1
        )

    def backward(i, carry):
        reward = jnp.sum(rwb[:, i, 0:1, :], axis=0)
        live = meta[8 + i, 1:2, :]
        pg = live * (jax.nn.sigmoid(reward) - meta[8 + i, 2:3, :])
        held = []
        for g in range(2):
            q2 = two(qgb, i, g, 0)
            go = two(qgb, i, g, 4 * D).astype(F32).T
            ga_t = jnp.concatenate(
                [
                    live * go[:, :T] + pg * rob[2 * g],
                    live * go[:, T:] + pg * rob[2 * g + 1],
                ],
                axis=1,
            ).astype(BF)
            ga_f = ga_t.astype(F32)
            part = inv[2 * i + g, 0:1, :]
            delta = jnp.sum(ga_f * ob[2 * i + g], axis=0, keepdims=True) * part
            ga2 = (ga_f * part).T.astype(BF)
            held.append((q2, ga_t, part, delta, ga2))

        def terms(g, j):
            q2, ga_t, part, delta, ga2 = held[g]
            at = slice(j * T, (j + 1) * T)
            here = rows((i + j) * T)
            low = pb[2 * i + g, at]
            dp = dot(kvb[here, (2 + g) * D : (3 + g) * D], ga_t, 1, 0)
            ds = (low.astype(F32) * (dp * part - delta)).astype(BF)
            dsb[g, at] = ds
            acc[here, g * D : (g + 1) * D] += dot(ds, q2, 1, 0)
            acc[here, (2 + g) * D : (3 + g) * D] += dot(low, ga2, 1, 0)

        for g in range(2):
            terms(g, 0)

        @pl.when(has2)
        def _():
            b2s[i] = packed(i * T).astype(BF)
            send(B2, b2s.at[i], b2r.at[i], dn, i, i)

        for g in range(2):
            for j in range(1, 9):
                terms(g, j)
            gq = dot(kvt[g * D : (g + 1) * D, win(i)], dsb[g], 1, 0) * SCALE
            gq = gq.T.astype(BF)
            gqb[i, :, 2 * g * D : (2 * g + 1) * D] = gq[:T]
            gqb[i, :, (2 * g + 1) * D : (2 * g + 2) * D] = gq[T:]

        @pl.when(i == r)
        def _():
            pltpu.make_async_copy(gqb.at[i], oq.at[i], rsem.at[OQ, i]).start()

        @pl.when(i != r)
        def _():
            send(OQ, gqb.at[i], oq.at[r], base + i, i, r)

        return carry

    lax.fori_loop(0, R, backward, 0)

    def near(c, carry):
        @pl.when(mid)
        def _():
            wait_recv(B2, c, b2r.at[c])
            b1s[c] = (packed((4 + c) * T) + b2r[c].astype(F32)).astype(BF)

        @pl.when(jnp.logical_and(has_dn, jnp.logical_not(has_up)))
        def _():
            b1s[c] = packed((4 + c) * T).astype(BF)

        @pl.when(has_dn)
        def _():
            send(B1, b1s.at[c], b1r.at[c], dn, c, c)

        return carry

    lax.fori_loop(0, R, near, 0)

    def own(c, carry):
        @pl.when(has_up)
        def _():
            wait_recv(B1, c, b1r.at[c])
            kvs[c] = (packed((8 + c) * T) + b1r[c].astype(F32)).astype(BF)

        @pl.when(jnp.logical_not(has_up))
        def _():
            kvs[c] = packed((8 + c) * T).astype(BF)

        @pl.when(c == r)
        def _():
            pltpu.make_async_copy(kvs.at[c], okv.at[c], rsem.at[OKV, c]).start()

        @pl.when(c != r)
        def _():
            send(OKV, kvs.at[c], okv.at[r], base + c, c, r)

        return carry

    lax.fori_loop(0, R, own, 0)

    for o in range(1, R):
        d = peer(o)
        wait_send(KV_A, d, kchunk(8))
        wait_send(ME_A, d, meta.at[8])
        wait_send(QG_A, d, qchunk(0))
        wait_send(RW, d, rwb.at[0])
        wait_send(OQ, d, gqb.at[0])
        wait_send(OKV, d, kvs.at[0])
    for c in range(R):
        @pl.when(has_up)
        def _():
            wait_send(KV_1, c, kchunk(8 + c))
            wait_send(ME_1, c, meta.at[8 + c])

        @pl.when(mid)
        def _():
            wait_send(KV_2, c, kchunk(4 + c))
            wait_send(ME_2, c, meta.at[4 + c])

        @pl.when(has2)
        def _():
            wait_send(B2, c, b2s.at[c])

        @pl.when(has_dn)
        def _():
            wait_send(B1, c, b1s.at[c])

        wait_recv(OQ, c, oq.at[c])
        wait_recv(OKV, c, okv.at[c])


def local(n, queries, keys, values, grad_out, readout, segments, loss_mask, labels):
    tokens, heads, dim = queries.shape
    kv = keys.shape[1]

    def parts(*arrays):
        flat = [a.reshape(tokens, R, -1) for a in arrays]
        return jnp.concatenate(flat, axis=2).transpose(1, 0, 2)

    kv_in = parts(keys, values)
    qg_in = parts(queries, grad_out)
    rows3 = [x.reshape(1, tokens) for x in (segments, loss_mask, labels)]
    any_spec = pl.BlockSpec(memory_space=pl.ANY)
    vmem = pltpu.VMEM
    span = WINDOW + R * T
    oq, okv = pl.pallas_call(
        functools.partial(kernel, n),
        out_shape=[
            jax.ShapeDtypeStruct((R, T, 4 * D), BF),
            jax.ShapeDtypeStruct((R, T, 4 * D), BF),
        ],
        in_specs=[any_spec, any_spec] + [pl.BlockSpec(memory_space=pltpu.VMEM)] * 4,
        out_specs=[any_spec, any_spec],
        scratch_shapes=[
            vmem((span, 4 * D), BF),
            vmem((R * T, 8 * D), BF),
            vmem((12, 8, T), F32),
            vmem((span, T), F32),
            vmem((4, D, D), F32),
            vmem((8, WINDOW + T, 2 * T), BF),
            vmem((8, D, 2 * T), F32),
            vmem((R, R, 8, T), F32),
            vmem((span, 4 * D), F32),
            vmem((R, T, 4 * D), BF),
            vmem((R, T, 4 * D), BF),
            vmem((R, T, 4 * D), BF),
            vmem((R, T, 4 * D), BF),
            vmem((R, T, 4 * D), BF),
            vmem((R, T, 4 * D), BF),
            vmem((8, T), F32),
            vmem((4 * D, span), BF),
            vmem((2, WINDOW + T, 2 * T), F32),
            vmem((2, WINDOW + T, 2 * T), BF),
            vmem((8, 8, 2 * T), F32),
            pltpu.SemaphoreType.DMA((12, R)),
            pltpu.SemaphoreType.DMA((12, R)),
        ],
        compiler_params=pltpu.CompilerParams(
            collective_id=0, has_side_effects=True, vmem_limit_bytes=48 * 1024 * 1024
        ),
    )(kv_in, qg_in, *rows3, readout)
    grad_queries = oq.transpose(1, 0, 2).reshape(tokens, heads, dim)
    both = okv.transpose(1, 0, 2)
    grad_keys = both[:, :, : 2 * D].reshape(tokens, kv, dim)
    grad_values = both[:, :, 2 * D :].reshape(tokens, kv, dim)
    return grad_queries, grad_keys, grad_values


def solution(mesh):
    tok = P(("groups", "context"), None, None)
    row = P(("groups", "context"))
    return jax.shard_map(
        functools.partial(local, mesh.shape["context"]),
        mesh=mesh,
        in_specs=(tok, tok, tok, tok, P(), row, row, row),
        out_specs=(tok, tok, tok),
        check_vma=False,
    )
```

```python
import functools

import jax
import jax.numpy as jnp
from jax import lax
from jax.experimental import pallas as pl
from jax.experimental.pallas import tpu as pltpu
from jax.sharding import PartitionSpec as P

WINDOW = 1024
SCALE = 168.0 ** (-0.5)
NEGATIVE = -1e30
LOG2E = 1.4426950408889634
MESH = pl.DeviceIdType.MESH
R = 4
T = 128
D = 128
BF = jnp.bfloat16
F32 = jnp.float32
KV_A, QG_A, ME_A, KV_1, ME_1, KV_2, ME_2, RW, B2, B1, OQ, OKV = range(12)


def dot(a, b, ca, cb):
    return lax.dot_general(a, b, (((ca,), (cb,)), ((), ())), preferred_element_type=F32)


def kernel(
    n, kv_in, qg_in, seg_ref, live_ref, lab_ref, ro_ref, oq, okv,
    kvb, qgb, meta, segc, rob, pb, ob, rwb, acc, gqb, b2s, b2r, b1s, b1r, kvs,
    me_in, kvt, sb, dsb, inv,
    ssem, rsem,
):
    planes = n // R
    me = lax.axis_index("context")
    r = lax.rem(me, R)
    p = lax.div(me, R)
    base = p * R
    has_dn = p >= 1
    has_up = p < planes - 1
    has2 = p >= 2
    mid = jnp.logical_and(has_dn, has_up)
    up = me + R
    dn = me - R

    def send(k, src, dst, to, s, d):
        pltpu.make_async_remote_copy(
            src_ref=src, dst_ref=dst, send_sem=ssem.at[k, s], recv_sem=rsem.at[k, d],
            device_id={"context": to}, device_id_type=MESH,
        ).start()

    def wait_recv(k, c, ref):
        pltpu.make_async_copy(ref, ref, rsem.at[k, c]).wait()

    def wait_send(k, c, ref):
        pltpu.make_async_copy(ref, ref, ssem.at[k, c]).wait()

    def peer(o):
        return lax.rem(r + o, R)

    def rows(start):
        return pl.ds(pl.multiple_of(start, T), T)

    def kchunk(c):
        return kvb.at[rows(c * T)]

    def qchunk(c):
        return qgb.at[rows(c * T)]

    barrier = pltpu.get_barrier_semaphore()
    for o in range(1, R):
        pl.semaphore_signal(barrier, inc=1, device_id={"context": base + peer(o)}, device_id_type=MESH)

    @pl.when(has_dn)
    def _():
        pl.semaphore_signal(barrier, inc=1, device_id={"context": dn}, device_id_type=MESH)

    @pl.when(has_up)
    def _():
        pl.semaphore_signal(barrier, inc=1, device_id={"context": up}, device_id_type=MESH)

    me_in[...] = jnp.concatenate(
        [seg_ref[...], live_ref[...], lab_ref[...], jnp.zeros((5, T), jnp.int32)], axis=0
    ).astype(F32)
    pltpu.make_async_copy(kv_in.at[r], kchunk(8 + r), rsem.at[KV_A, r]).start()
    pltpu.make_async_copy(me_in, meta.at[8 + r], rsem.at[ME_A, r]).start()
    pltpu.make_async_copy(qg_in.at[r], qchunk(r), rsem.at[QG_A, r]).start()
    pl.semaphore_wait(barrier, R - 1 + has_dn.astype(jnp.int32) + has_up.astype(jnp.int32))

    for o in range(1, R):
        d = peer(o)
        send(KV_A, kv_in.at[d], kchunk(8 + r), base + d, d, r)
        send(ME_A, me_in, meta.at[8 + r], base + d, d, r)
    for k in range(R):
        c = lax.rem(5 - k + 2 * lax.div(r, 2), R)
        wait_recv(KV_A, c, kchunk(8 + c))
        wait_recv(ME_A, c, meta.at[8 + c])

        @pl.when(has_up)
        def _():
            send(KV_1, kchunk(8 + c), kchunk(4 + c), up, c, c)
            send(ME_1, meta.at[8 + c], meta.at[4 + c], up, c, c)

    for o in range(1, R):
        d = peer(o)
        send(QG_A, qg_in.at[d], qchunk(r), base + d, d, r)

    @pl.when(jnp.logical_not(has_dn))
    def _():
        kvb[4 * T : 8 * T] = jnp.zeros((4 * T, 4 * D), BF)
        meta[4:8] = jnp.full((4, 8, T), -1.0, F32)

    @pl.when(jnp.logical_not(has2))
    def _():
        kvb[0 : 4 * T] = jnp.zeros((4 * T, 4 * D), BF)
        meta[0:4] = jnp.full((4, 8, T), -1.0, F32)

    acc[...] = jnp.zeros_like(acc)
    for h in range(4):
        rob[h] = jnp.broadcast_to(ro_ref[pl.ds(4 * r + h, 1), :], (D, D)).T

    for c in range(R - 1, -1, -1):
        @pl.when(has_dn)
        def _():
            wait_recv(KV_1, c, kchunk(4 + c))
            wait_recv(ME_1, c, meta.at[4 + c])

        @pl.when(mid)
        def _():
            send(KV_2, kchunk(4 + c), kchunk(c), up, c, c)
            send(ME_2, meta.at[4 + c], meta.at[c], up, c, c)

    for c in range(R):
        wait_recv(QG_A, c, qchunk(c))

    def seg_column(c):
        segc[rows(c * T)] = jnp.broadcast_to(meta[c, 0:1, :], (T, T)).T
        kvt[:, rows(c * T)] = kvb[rows(c * T)].T

    def seg_body(c, carry):
        seg_column(c + 4)
        return carry

    lax.fori_loop(0, 8, seg_body, 0)

    def win(i):
        return pl.ds(pl.multiple_of(i * T, T), WINDOW + T)

    def two(ref, i, g, at):
        lane = at + 2 * g * D
        return jnp.concatenate(
            [ref[rows(i * T), lane : lane + D], ref[rows(i * T), lane + D : lane + 2 * D]], axis=0
        )

    def forward(step, carry):
        i = R - 1 - step

        seg_q = meta[8 + i, 0:1, :]
        q2s = [two(qgb, i, g, 0) for g in range(2)]

        def scores(j, tops):
            at = slice(j * T, (j + 1) * T)
            ok = segc[rows((i + j) * T)] == seg_q
            if j in (0, 8):
                kk = lax.broadcasted_iota(jnp.int32, (T, T), 0)
                tq = lax.broadcasted_iota(jnp.int32, (T, T), 1)
                ok = jnp.logical_and(ok, kk > tq if j == 0 else kk <= tq)
            b = jnp.where(ok, 0.0, NEGATIVE)
            b = jnp.concatenate([b, b], axis=1)
            new = []
            for g in range(2):
                raw = dot(kvb[rows((i + j) * T), g * D : (g + 1) * D], q2s[g], 1, 1)
                x = raw * (SCALE * LOG2E) + b
                sb[g, at] = x
                m = jnp.max(x.reshape(T // 8, 8, 2 * T), axis=0)
                new.append(jnp.maximum(tops[g], m))
            return new

        tops = [jnp.full((8, 2 * T), 2 * NEGATIVE, F32)] * 2
        for j in range(1, 9):
            tops = scores(j, tops)

        @pl.when(has2)
        def _():
            wait_recv(KV_2, i, kchunk(i))
            wait_recv(ME_2, i, meta.at[i])

        seg_column(i)
        tops = scores(0, tops)
        total = jnp.zeros((1, T), F32)
        for g in range(2):
            top = tops[g]
            top = jnp.max(top, axis=0, keepdims=True)
            total_e = None
            for j in range(9):
                at = slice(j * T, (j + 1) * T)
                e = jnp.exp2(sb[g, at] - top)
                pb[2 * i + g, at] = e.astype(BF)
                m = jnp.sum(e.reshape(T // 8, 8, 2 * T), axis=0)
                total_e = m if total_e is None else total_e + m
            part = 1.0 / jnp.sum(total_e, axis=0, keepdims=True)
            inv[2 * i + g] = jnp.broadcast_to(part, (8, 2 * T))
            vt = kvt[(2 + g) * D : (3 + g) * D, win(i)]
            o = dot(vt, pb[2 * i + g], 1, 0) * part
            ob[2 * i + g] = o
            w = o[:, :T] * rob[2 * g] + o[:, T:] * rob[2 * g + 1]
            total = total + jnp.sum(w, axis=0, keepdims=True)
        rwb[r, i] = jnp.broadcast_to(total, (8, T))
        return carry

    lax.fori_loop(0, R, forward, 0)

    for o in range(1, R):
        send(RW, rwb.at[r], rwb.at[r], base + peer(o), peer(o), r)
    for o in range(1, R):
        wait_recv(RW, peer(o), rwb.at[peer(o)])

    def packed(start):
        return jnp.concatenate(
            [acc[rows(start), : 2 * D] * SCALE, acc[rows(start), 2 * D :]], axis=1
        )

    def near(c):
        @pl.when(mid)
        def _():
            wait_recv(B2, c, b2r.at[c])
            b1s[c] = (packed((4 + c) * T) + b2r[c].astype(F32)).astype(BF)

        @pl.when(jnp.logical_and(has_dn, jnp.logical_not(has_up)))
        def _():
            b1s[c] = packed((4 + c) * T).astype(BF)

        @pl.when(has_dn)
        def _():
            send(B1, b1s.at[c], b1r.at[c], dn, c, c)

    def backward(i, carry):
        reward = jnp.sum(rwb[:, i, 0:1, :], axis=0)
        live = meta[8 + i, 1:2, :]
        pg = live * (jax.nn.sigmoid(reward) - meta[8 + i, 2:3, :])
        held = []
        for g in range(2):
            q2 = two(qgb, i, g, 0)
            go = two(qgb, i, g, 4 * D).astype(F32).T
            ga_t = jnp.concatenate(
                [
                    live * go[:, :T] + pg * rob[2 * g],
                    live * go[:, T:] + pg * rob[2 * g + 1],
                ],
                axis=1,
            ).astype(BF)
            ga_f = ga_t.astype(F32)
            part = inv[2 * i + g, 0:1, :]
            delta = jnp.sum(ga_f * ob[2 * i + g], axis=0, keepdims=True) * part
            ga2 = (ga_f * part).T.astype(BF)
            held.append((q2, ga_t, part, delta, ga2))

        def terms(g, j):
            q2, ga_t, part, delta, ga2 = held[g]
            at = slice(j * T, (j + 1) * T)
            here = rows((i + j) * T)
            low = pb[2 * i + g, at]
            dp = dot(kvb[here, (2 + g) * D : (3 + g) * D], ga_t, 1, 0)
            ds = (low.astype(F32) * (dp * part - delta)).astype(BF)
            dsb[g, at] = ds
            acc[here, g * D : (g + 1) * D] += dot(ds, q2, 1, 0)
            acc[here, (2 + g) * D : (3 + g) * D] += dot(low, ga2, 1, 0)

        for g in range(2):
            terms(g, 0)

        @pl.when(has2)
        def _():
            b2s[i] = packed(i * T).astype(BF)
            send(B2, b2s.at[i], b2r.at[i], dn, i, i)

        for span, ready in ((range(1, 5), (0, 1)), (range(5, 7), (2,)), (range(7, 9), (3,))):
            for j in span:
                for g in range(2):
                    terms(g, j)

            @pl.when(i == R - 1)
            def _():
                for c in ready:
                    near(c)

        for g in range(2):
            gq = dot(kvt[g * D : (g + 1) * D, win(i)], dsb[g], 1, 0) * SCALE
            gq = gq.T.astype(BF)
            gqb[i, :, 2 * g * D : (2 * g + 1) * D] = gq[:T]
            gqb[i, :, (2 * g + 1) * D : (2 * g + 2) * D] = gq[T:]

        @pl.when(i == r)
        def _():
            pltpu.make_async_copy(gqb.at[i], oq.at[i], rsem.at[OQ, i]).start()

        @pl.when(i != r)
        def _():
            send(OQ, gqb.at[i], oq.at[r], base + i, i, r)

        return carry

    lax.fori_loop(0, R, backward, 0)

    def own(c, carry):
        @pl.when(has_up)
        def _():
            wait_recv(B1, c, b1r.at[c])
            kvs[c] = (packed((8 + c) * T) + b1r[c].astype(F32)).astype(BF)

        @pl.when(jnp.logical_not(has_up))
        def _():
            kvs[c] = packed((8 + c) * T).astype(BF)

        @pl.when(c == r)
        def _():
            pltpu.make_async_copy(kvs.at[c], okv.at[c], rsem.at[OKV, c]).start()

        @pl.when(c != r)
        def _():
            send(OKV, kvs.at[c], okv.at[r], base + c, c, r)

        return carry

    lax.fori_loop(0, R, own, 0)

    for o in range(1, R):
        d = peer(o)
        wait_send(KV_A, d, kchunk(8))
        wait_send(ME_A, d, meta.at[8])
        wait_send(QG_A, d, qchunk(0))
        wait_send(RW, d, rwb.at[0])
        wait_send(OQ, d, gqb.at[0])
        wait_send(OKV, d, kvs.at[0])
    for c in range(R):
        @pl.when(has_up)
        def _():
            wait_send(KV_1, c, kchunk(8 + c))
            wait_send(ME_1, c, meta.at[8 + c])

        @pl.when(mid)
        def _():
            wait_send(KV_2, c, kchunk(4 + c))
            wait_send(ME_2, c, meta.at[4 + c])

        @pl.when(has2)
        def _():
            wait_send(B2, c, b2s.at[c])

        @pl.when(has_dn)
        def _():
            wait_send(B1, c, b1s.at[c])

        wait_recv(OQ, c, oq.at[c])
        wait_recv(OKV, c, okv.at[c])


def local(n, queries, keys, values, grad_out, readout, segments, loss_mask, labels):
    tokens, heads, dim = queries.shape
    kv = keys.shape[1]

    def parts(*arrays):
        flat = [a.reshape(tokens, R, -1) for a in arrays]
        return jnp.concatenate(flat, axis=2).transpose(1, 0, 2)

    kv_in = parts(keys, values)
    qg_in = parts(queries, grad_out)
    rows3 = [x.reshape(1, tokens) for x in (segments, loss_mask, labels)]
    any_spec = pl.BlockSpec(memory_space=pl.ANY)
    vmem = pltpu.VMEM
    span = WINDOW + R * T
    oq, okv = pl.pallas_call(
        functools.partial(kernel, n),
        out_shape=[
            jax.ShapeDtypeStruct((R, T, 4 * D), BF),
            jax.ShapeDtypeStruct((R, T, 4 * D), BF),
        ],
        in_specs=[any_spec, any_spec] + [pl.BlockSpec(memory_space=pltpu.VMEM)] * 4,
        out_specs=[any_spec, any_spec],
        scratch_shapes=[
            vmem((span, 4 * D), BF),
            vmem((R * T, 8 * D), BF),
            vmem((12, 8, T), F32),
            vmem((span, T), F32),
            vmem((4, D, D), F32),
            vmem((8, WINDOW + T, 2 * T), BF),
            vmem((8, D, 2 * T), F32),
            vmem((R, R, 8, T), F32),
            vmem((span, 4 * D), F32),
            vmem((R, T, 4 * D), BF),
            vmem((R, T, 4 * D), BF),
            vmem((R, T, 4 * D), BF),
            vmem((R, T, 4 * D), BF),
            vmem((R, T, 4 * D), BF),
            vmem((R, T, 4 * D), BF),
            vmem((8, T), F32),
            vmem((4 * D, span), BF),
            vmem((2, WINDOW + T, 2 * T), F32),
            vmem((2, WINDOW + T, 2 * T), BF),
            vmem((8, 8, 2 * T), F32),
            pltpu.SemaphoreType.DMA((12, R)),
            pltpu.SemaphoreType.DMA((12, R)),
        ],
        compiler_params=pltpu.CompilerParams(
            collective_id=0, has_side_effects=True, vmem_limit_bytes=48 * 1024 * 1024
        ),
    )(kv_in, qg_in, *rows3, readout)
    grad_queries = oq.transpose(1, 0, 2).reshape(tokens, heads, dim)
    both = okv.transpose(1, 0, 2)
    grad_keys = both[:, :, : 2 * D].reshape(tokens, kv, dim)
    grad_values = both[:, :, 2 * D :].reshape(tokens, kv, dim)
    return grad_queries, grad_keys, grad_values


def solution(mesh):
    tok = P(("groups", "context"), None, None)
    row = P(("groups", "context"))
    return jax.shard_map(
        functools.partial(local, mesh.shape["context"]),
        mesh=mesh,
        in_specs=(tok, tok, tok, tok, P(), row, row, row),
        out_specs=(tok, tok, tok),
        check_vma=False,
    )
```

```python
import functools

import jax
import jax.numpy as jnp
from jax import lax
from jax.experimental import pallas as pl
from jax.experimental.pallas import tpu as pltpu
from jax.sharding import PartitionSpec as P

WINDOW = 1024
SCALE = 168.0 ** (-0.5)
NEGATIVE = -1e30
LOG2E = 1.4426950408889634
MESH = pl.DeviceIdType.MESH
R = 4
T = 128
D = 128
BF = jnp.bfloat16
F32 = jnp.float32
KV_A, QG_A, ME_A, KV_1, ME_1, KV_2, ME_2, RW, B2, B1, OQ, OKV = range(12)


def dot(a, b, ca, cb):
    return lax.dot_general(a, b, (((ca,), (cb,)), ((), ())), preferred_element_type=F32)


def kernel(
    n, kv_in, qg_in, seg_ref, live_ref, lab_ref, ro_ref, oq, okv,
    kvb, qgb, meta, segc, rob, pb, ob, rwb, acc, gqb, b2s, b2r, b1s, b1r, kvs,
    me_in, kvt, sb, dsb, inv,
    ssem, rsem,
):
    planes = n // R
    me = lax.axis_index("context")
    r = lax.rem(me, R)
    p = lax.div(me, R)
    base = p * R
    has_dn = p >= 1
    has_up = p < planes - 1
    has2 = p >= 2
    mid = jnp.logical_and(has_dn, has_up)
    up = me + R
    dn = me - R

    def send(k, src, dst, to, s, d):
        pltpu.make_async_remote_copy(
            src_ref=src, dst_ref=dst, send_sem=ssem.at[k, s], recv_sem=rsem.at[k, d],
            device_id={"context": to}, device_id_type=MESH,
        ).start()

    def wait_recv(k, c, ref):
        pltpu.make_async_copy(ref, ref, rsem.at[k, c]).wait()

    def wait_send(k, c, ref):
        pltpu.make_async_copy(ref, ref, ssem.at[k, c]).wait()

    def peer(o):
        return lax.rem(r + o, R)

    def rows(start):
        return pl.ds(pl.multiple_of(start, T), T)

    def kchunk(c):
        return kvb.at[rows(c * T)]

    def qchunk(c):
        return qgb.at[rows(c * T)]

    barrier = pltpu.get_barrier_semaphore()
    for o in range(1, R):
        pl.semaphore_signal(barrier, inc=1, device_id={"context": base + peer(o)}, device_id_type=MESH)

    @pl.when(has_dn)
    def _():
        pl.semaphore_signal(barrier, inc=1, device_id={"context": dn}, device_id_type=MESH)

    @pl.when(has_up)
    def _():
        pl.semaphore_signal(barrier, inc=1, device_id={"context": up}, device_id_type=MESH)

    me_in[...] = jnp.concatenate(
        [seg_ref[...], live_ref[...], lab_ref[...], jnp.zeros((5, T), jnp.int32)], axis=0
    ).astype(F32)
    pltpu.make_async_copy(kv_in.at[r], kchunk(8 + r), rsem.at[KV_A, r]).start()
    pltpu.make_async_copy(me_in, meta.at[8 + r], rsem.at[ME_A, r]).start()
    pltpu.make_async_copy(qg_in.at[r], qchunk(r), rsem.at[QG_A, r]).start()
    pl.semaphore_wait(barrier, R - 1 + has_dn.astype(jnp.int32) + has_up.astype(jnp.int32))

    for o in range(1, R):
        d = peer(o)
        send(KV_A, kv_in.at[d], kchunk(8 + r), base + d, d, r)
        send(ME_A, me_in, meta.at[8 + r], base + d, d, r)
    for k in range(R):
        c = lax.rem(5 - k + 2 * lax.div(r, 2), R)
        wait_recv(KV_A, c, kchunk(8 + c))
        wait_recv(ME_A, c, meta.at[8 + c])

        @pl.when(has_up)
        def _():
            send(KV_1, kchunk(8 + c), kchunk(4 + c), up, c, c)
            send(ME_1, meta.at[8 + c], meta.at[4 + c], up, c, c)

    for o in range(1, R):
        d = peer(o)
        send(QG_A, qg_in.at[d], qchunk(r), base + d, d, r)

    @pl.when(jnp.logical_not(has_dn))
    def _():
        kvb[4 * T : 8 * T] = jnp.zeros((4 * T, 4 * D), BF)
        meta[4:8] = jnp.full((4, 8, T), -1.0, F32)

    @pl.when(jnp.logical_not(has2))
    def _():
        kvb[0 : 4 * T] = jnp.zeros((4 * T, 4 * D), BF)
        meta[0:4] = jnp.full((4, 8, T), -1.0, F32)

    acc[...] = jnp.zeros_like(acc)
    for h in range(4):
        rob[h] = jnp.broadcast_to(ro_ref[pl.ds(4 * r + h, 1), :], (D, D)).T

    for c in range(R - 1, -1, -1):
        @pl.when(has_dn)
        def _():
            wait_recv(KV_1, c, kchunk(4 + c))
            wait_recv(ME_1, c, meta.at[4 + c])

        @pl.when(mid)
        def _():
            send(KV_2, kchunk(4 + c), kchunk(c), up, c, c)
            send(ME_2, meta.at[4 + c], meta.at[c], up, c, c)

    for c in range(R):
        wait_recv(QG_A, c, qchunk(c))

    def seg_column(c):
        segc[rows(c * T)] = jnp.broadcast_to(meta[c, 0:1, :], (T, T)).T
        kvt[:, rows(c * T)] = kvb[rows(c * T)].T

    def seg_body(c, carry):
        seg_column(c + 4)
        return carry

    lax.fori_loop(0, 8, seg_body, 0)

    def win(i):
        return pl.ds(pl.multiple_of(i * T, T), WINDOW + T)

    def two(ref, i, g, at):
        lane = at + 2 * g * D
        return jnp.concatenate(
            [ref[rows(i * T), lane : lane + D], ref[rows(i * T), lane + D : lane + 2 * D]], axis=0
        )

    def forward(step, carry):
        i = R - 1 - step

        seg_q = meta[8 + i, 0:1, :]
        q2s = [two(qgb, i, g, 0) for g in range(2)]

        def scores(j, tops):
            at = slice(j * T, (j + 1) * T)
            ok = segc[rows((i + j) * T)] == seg_q
            if j in (0, 8):
                kk = lax.broadcasted_iota(jnp.int32, (T, T), 0)
                tq = lax.broadcasted_iota(jnp.int32, (T, T), 1)
                ok = jnp.logical_and(ok, kk > tq if j == 0 else kk <= tq)
            b = jnp.where(ok, 0.0, NEGATIVE)
            b = jnp.concatenate([b, b], axis=1)
            new = []
            for g in range(2):
                raw = dot(kvb[rows((i + j) * T), g * D : (g + 1) * D], q2s[g], 1, 1)
                x = raw * (SCALE * LOG2E) + b
                sb[g, at] = x
                m = jnp.max(x.reshape(T // 8, 8, 2 * T), axis=0)
                new.append(jnp.maximum(tops[g], m))
            return new

        tops = [jnp.full((8, 2 * T), 2 * NEGATIVE, F32)] * 2
        for j in range(1, 9):
            tops = scores(j, tops)
        rest = []
        for g in range(2):
            top = jnp.max(tops[g], axis=0, keepdims=True)
            total_e = jnp.zeros((8, 2 * T), F32)
            for j in range(1, 9):
                at = slice(j * T, (j + 1) * T)
                e = jnp.exp2(sb[g, at] - top)
                pb[2 * i + g, at] = e.astype(BF)
                total_e = total_e + jnp.sum(e.reshape(T // 8, 8, 2 * T), axis=0)
            vt = kvt[(2 + g) * D : (3 + g) * D, pl.ds(pl.multiple_of((i + 1) * T, T), WINDOW)]
            o = dot(vt, pb[2 * i + g, T:], 1, 0)
            rest.append((top, jnp.sum(total_e, axis=0, keepdims=True), o))

        @pl.when(has2)
        def _():
            wait_recv(KV_2, i, kchunk(i))
            wait_recv(ME_2, i, meta.at[i])

        seg_column(i)
        tops = scores(0, tops)
        total = jnp.zeros((1, T), F32)
        for g in range(2):
            old, old_sum, old_o = rest[g]
            top = jnp.max(tops[g], axis=0, keepdims=True)
            shrink = jnp.exp2(old - top)
            e = jnp.exp2(sb[g, :T] - top)
            low = e.astype(BF)
            pb[2 * i + g, :T] = low
            far = 1.0 / (old_sum * shrink + jnp.sum(e, axis=0, keepdims=True))
            part = far * shrink
            inv[2 * i + g] = jnp.broadcast_to(part, (8, 2 * T))
            inv[8 + 2 * i + g] = jnp.broadcast_to(far, (8, 2 * T))
            vt = kvt[(2 + g) * D : (3 + g) * D, rows(i * T)]
            o = old_o * part + dot(vt, low, 1, 0) * far
            ob[2 * i + g] = o
            w = o[:, :T] * rob[2 * g] + o[:, T:] * rob[2 * g + 1]
            total = total + jnp.sum(w, axis=0, keepdims=True)
        rwb[r, i] = jnp.broadcast_to(total, (8, T))
        return carry

    lax.fori_loop(0, R, forward, 0)

    for o in range(1, R):
        send(RW, rwb.at[r], rwb.at[r], base + peer(o), peer(o), r)
    for o in range(1, R):
        wait_recv(RW, peer(o), rwb.at[peer(o)])

    def packed(start):
        return jnp.concatenate(
            [acc[rows(start), : 2 * D] * SCALE, acc[rows(start), 2 * D :]], axis=1
        )

    def backward(i, carry):
        reward = jnp.sum(rwb[:, i, 0:1, :], axis=0)
        live = meta[8 + i, 1:2, :]
        pg = live * (jax.nn.sigmoid(reward) - meta[8 + i, 2:3, :])
        held = []
        for g in range(2):
            q2 = two(qgb, i, g, 0)
            go = two(qgb, i, g, 4 * D).astype(F32).T
            ga_t = jnp.concatenate(
                [
                    live * go[:, :T] + pg * rob[2 * g],
                    live * go[:, T:] + pg * rob[2 * g + 1],
                ],
                axis=1,
            ).astype(BF)
            ga_f = ga_t.astype(F32)
            part = inv[2 * i + g, 0:1, :]
            far = inv[8 + 2 * i + g, 0:1, :]
            delta = jnp.sum(ga_f * ob[2 * i + g], axis=0, keepdims=True)
            ga2 = (ga_f * part).T.astype(BF)
            ga0 = (ga_f * far).T.astype(BF)
            held.append((q2, ga_t, (far, part), delta, (ga0, ga2)))

        def terms(g, j):
            q2, ga_t, parts, delta, gas = held[g]
            part, ga2 = parts[min(j, 1)], gas[min(j, 1)]
            at = slice(j * T, (j + 1) * T)
            here = rows((i + j) * T)
            low = pb[2 * i + g, at]
            dp = dot(kvb[here, (2 + g) * D : (3 + g) * D], ga_t, 1, 0)
            ds = (low.astype(F32) * ((dp - delta) * part)).astype(BF)
            dsb[g, at] = ds
            acc[here, g * D : (g + 1) * D] += dot(ds, q2, 1, 0)
            acc[here, (2 + g) * D : (3 + g) * D] += dot(low, ga2, 1, 0)

        for g in range(2):
            terms(g, 0)

        @pl.when(has2)
        def _():
            b2s[i] = packed(i * T).astype(BF)
            send(B2, b2s.at[i], b2r.at[i], dn, i, i)

        for g in range(2):
            for j in range(1, 9):
                terms(g, j)
            gq = dot(kvt[g * D : (g + 1) * D, win(i)], dsb[g], 1, 0) * SCALE
            gq = gq.T.astype(BF)
            gqb[i, :, 2 * g * D : (2 * g + 1) * D] = gq[:T]
            gqb[i, :, (2 * g + 1) * D : (2 * g + 2) * D] = gq[T:]

        @pl.when(i == r)
        def _():
            pltpu.make_async_copy(gqb.at[i], oq.at[i], rsem.at[OQ, i]).start()

        @pl.when(i != r)
        def _():
            send(OQ, gqb.at[i], oq.at[r], base + i, i, r)

        return carry

    lax.fori_loop(0, R, backward, 0)

    def near(c, carry):
        @pl.when(mid)
        def _():
            wait_recv(B2, c, b2r.at[c])
            b1s[c] = (packed((4 + c) * T) + b2r[c].astype(F32)).astype(BF)

        @pl.when(jnp.logical_and(has_dn, jnp.logical_not(has_up)))
        def _():
            b1s[c] = packed((4 + c) * T).astype(BF)

        @pl.when(has_dn)
        def _():
            send(B1, b1s.at[c], b1r.at[c], dn, c, c)

        return carry

    lax.fori_loop(0, R, near, 0)

    def own(c, carry):
        @pl.when(has_up)
        def _():
            wait_recv(B1, c, b1r.at[c])
            kvs[c] = (packed((8 + c) * T) + b1r[c].astype(F32)).astype(BF)

        @pl.when(jnp.logical_not(has_up))
        def _():
            kvs[c] = packed((8 + c) * T).astype(BF)

        @pl.when(c == r)
        def _():
            pltpu.make_async_copy(kvs.at[c], okv.at[c], rsem.at[OKV, c]).start()

        @pl.when(c != r)
        def _():
            send(OKV, kvs.at[c], okv.at[r], base + c, c, r)

        return carry

    lax.fori_loop(0, R, own, 0)

    for o in range(1, R):
        d = peer(o)
        wait_send(KV_A, d, kchunk(8))
        wait_send(ME_A, d, meta.at[8])
        wait_send(QG_A, d, qchunk(0))
        wait_send(RW, d, rwb.at[0])
        wait_send(OQ, d, gqb.at[0])
        wait_send(OKV, d, kvs.at[0])
    for c in range(R):
        @pl.when(has_up)
        def _():
            wait_send(KV_1, c, kchunk(8 + c))
            wait_send(ME_1, c, meta.at[8 + c])

        @pl.when(mid)
        def _():
            wait_send(KV_2, c, kchunk(4 + c))
            wait_send(ME_2, c, meta.at[4 + c])

        @pl.when(has2)
        def _():
            wait_send(B2, c, b2s.at[c])

        @pl.when(has_dn)
        def _():
            wait_send(B1, c, b1s.at[c])

        wait_recv(OQ, c, oq.at[c])
        wait_recv(OKV, c, okv.at[c])


def local(n, queries, keys, values, grad_out, readout, segments, loss_mask, labels):
    tokens, heads, dim = queries.shape
    kv = keys.shape[1]

    def parts(*arrays):
        flat = [a.reshape(tokens, R, -1) for a in arrays]
        return jnp.concatenate(flat, axis=2).transpose(1, 0, 2)

    kv_in = parts(keys, values)
    qg_in = parts(queries, grad_out)
    rows3 = [x.reshape(1, tokens) for x in (segments, loss_mask, labels)]
    any_spec = pl.BlockSpec(memory_space=pl.ANY)
    vmem = pltpu.VMEM
    span = WINDOW + R * T
    oq, okv = pl.pallas_call(
        functools.partial(kernel, n),
        out_shape=[
            jax.ShapeDtypeStruct((R, T, 4 * D), BF),
            jax.ShapeDtypeStruct((R, T, 4 * D), BF),
        ],
        in_specs=[any_spec, any_spec] + [pl.BlockSpec(memory_space=pltpu.VMEM)] * 4,
        out_specs=[any_spec, any_spec],
        scratch_shapes=[
            vmem((span, 4 * D), BF),
            vmem((R * T, 8 * D), BF),
            vmem((12, 8, T), F32),
            vmem((span, T), F32),
            vmem((4, D, D), F32),
            vmem((8, WINDOW + T, 2 * T), BF),
            vmem((8, D, 2 * T), F32),
            vmem((R, R, 8, T), F32),
            vmem((span, 4 * D), F32),
            vmem((R, T, 4 * D), BF),
            vmem((R, T, 4 * D), BF),
            vmem((R, T, 4 * D), BF),
            vmem((R, T, 4 * D), BF),
            vmem((R, T, 4 * D), BF),
            vmem((R, T, 4 * D), BF),
            vmem((8, T), F32),
            vmem((4 * D, span), BF),
            vmem((2, WINDOW + T, 2 * T), F32),
            vmem((2, WINDOW + T, 2 * T), BF),
            vmem((16, 8, 2 * T), F32),
            pltpu.SemaphoreType.DMA((12, R)),
            pltpu.SemaphoreType.DMA((12, R)),
        ],
        compiler_params=pltpu.CompilerParams(
            collective_id=0, has_side_effects=True, vmem_limit_bytes=48 * 1024 * 1024
        ),
    )(kv_in, qg_in, *rows3, readout)
    grad_queries = oq.transpose(1, 0, 2).reshape(tokens, heads, dim)
    both = okv.transpose(1, 0, 2)
    grad_keys = both[:, :, : 2 * D].reshape(tokens, kv, dim)
    grad_values = both[:, :, 2 * D :].reshape(tokens, kv, dim)
    return grad_queries, grad_keys, grad_values


def solution(mesh):
    tok = P(("groups", "context"), None, None)
    row = P(("groups", "context"))
    return jax.shard_map(
        functools.partial(local, mesh.shape["context"]),
        mesh=mesh,
        in_specs=(tok, tok, tok, tok, P(), row, row, row),
        out_specs=(tok, tok, tok),
        check_vma=False,
    )
```
